32 devices in a mesh: section: 2 (over core), seq: 4 (over y, x), fsdp: 4 (over z).
Axes of the slice: x: 2, y: 2, z: 4, core: 2. Of those that a mesh axis runs over, the one named last changes fastest.
Arguments:
- inputs: bfloat16 [2, 8, 1024, 1152], P(None, 'fsdp', 'seq'), may hold values from -6 to 6
- cotangent: bfloat16 [2, 8, 1024, 1152], P(None, 'fsdp', 'seq'), may hold values from -6 to 6
- segments: int32 [2, 8, 1024], P(None, 'fsdp', 'seq'), may hold values from 0 to 64, as said below
- w_query: bfloat16 [2, 1152, 1152], P('section', ('seq', 'fsdp')), may hold values from -0.1875 to 0.1875
- w_key: bfloat16 [2, 1152, 384], P('section', ('seq', 'fsdp')), may hold values from -0.1875 to 0.1875
- w_value: bfloat16 [2, 1152, 384], P('section', ('seq', 'fsdp')), may hold values from -0.1875 to 0.1875
- w_out: bfloat16 [2, 1152, 1152], P('section', None, ('seq', 'fsdp')), may hold values from -0.75 to 0.75
- w_gate: bfloat16 [2, 1152, 3072], P('section', ('seq', 'fsdp')), may hold values from -0.1875 to 0.1875
- w_up: bfloat16 [2, 1152, 3072], P('section', ('seq', 'fsdp')), may hold values from -0.1875 to 0.1875
- w_down: bfloat16 [2, 3072, 1152], P('section', None, ('seq', 'fsdp')), may hold values from -0.109375 to 0.109375
- norm_attn: bfloat16 [2, 1152], P('section', ('seq', 'fsdp')), may hold values from 0.25 to 1.75
- norm_mlp: bfloat16 [2, 1152], P('section', ('seq', 'fsdp')), may hold values from 0.25 to 1.75
Outputs:
- layer_out: bfloat16 [2, 2, 8, 1024, 1152], P('section', None, 'fsdp', 'seq')
- input_grad: bfloat16 [2, 2, 8, 1024, 1152], P('section', None, 'fsdp', 'seq')
- g_query: float32 [2, 1152, 1152], P('section', ('seq', 'fsdp'))
- g_key: float32 [2, 1152, 384], P('section', ('seq', 'fsdp'))
- g_value: float32 [2, 1152, 384], P('section', ('seq', 'fsdp'))
- g_out: float32 [2, 1152, 1152], P('section', None, ('seq', 'fsdp'))
- g_gate: float32 [2, 1152, 3072], P('section', ('seq', 'fsdp'))
- g_up: float32 [2, 1152, 3072], P('section', ('seq', 'fsdp'))
- g_down: float32 [2, 3072, 1152], P('section', None, ('seq', 'fsdp'))
- g_norm_attn: float32 [2, 1152], P('section', ('seq', 'fsdp'))
- g_norm_mlp: float32 [2, 1152], P('section', ('seq', 'fsdp'))
The draws below stay inside these ranges and needn't reach their ends.
Inputs may be any that keep to these rules, and one draw needn't show every extreme that they name: `segments`: within a sequence the numbers never fall except into a trailing run of 0 (the masked tail, at most a quarter of the sequence); documents are numbered 1, 2, ... in order. In every micro-batch, on every index of fsdp, one of its 2 sequences is a single document 1 with no tail.
All inputs are finite; a program needn't handle non-finite values.
Results may differ from the reference program's by a relative error of at most 0.038.
Values may be sent and summed in bfloat16 or wider, within the bound.
No kernel may reach another device: no remote copies, remote signals or barrier semaphores. Data moves between devices by JAX's collectives and lax.ppermute only.
A program may use at most 512 MiB of HBM per device.

```python
import jax
import jax.numpy as jnp
from jax import lax

D = 1152
KEY_VALUE_HEADS = 6
HEAD_SIZE = 64
FF = 3072
MB = 2
SEQ_DEV = 2
LENGTH = 1024
SEQ_FS = 8
QW = 1152
KW = 384
N_FSDP = 4


def draw_segments(key, part):
    key = jax.random.fold_in(key, 11)
    key_rate, key_tail, key_roll, key_pick = jax.random.split(key, 4)
    seq_total = MB * SEQ_FS
    doc_cap = min(64, LENGTH // 4)
    spacing = max(LENGTH // 128, 1)
    rate = 2 ** jax.random.randint(key_rate, (seq_total, 1), 0, 7)
    tail_len = jax.random.randint(key_tail, (seq_total, 1), 0, LENGTH // 4 + 1)
    rolls = jax.random.randint(key_roll, (seq_total, LENGTH), 0, LENGTH)
    position = jnp.arange(LENGTH)[None, :]
    chosen = jax.random.randint(key_pick, (MB, N_FSDP, 1), 0, SEQ_DEV)
    local_seq = jnp.arange(SEQ_DEV)[None, None, :]
    whole_doc = (local_seq == chosen).reshape(seq_total, 1)
    busy_local = (chosen[0, 0, 0] + 1) % SEQ_DEV
    seq_number = jnp.arange(seq_total)[:, None]
    busy = (seq_number == busy_local) & jnp.logical_not(whole_doc)
    forced = busy & (position % spacing == 0)
    cuts = (((rolls < rate) | forced) & (position > 0)).astype(jnp.int32)
    doc_ids = jnp.minimum(1 + jnp.cumsum(cuts, axis=1), doc_cap)
    doc_ids = jnp.where(position < LENGTH - tail_len, doc_ids, 0)
    doc_ids = jnp.where(whole_doc, 1, doc_ids)
    return doc_ids.reshape(MB, SEQ_FS, LENGTH).astype(jnp.int32)


def levels(key, dims, shards, least, high):
    def one(dim, parts):
        steps = jax.random.uniform(jax.random.fold_in(jax.random.fold_in(key, 6), dim), (parts,), jnp.float32, least / len(shards), high / len(shards))
        return jnp.repeat(jnp.exp(steps), dims[dim] // parts).reshape((-1,) + (1,) * (len(dims) - dim - 1))

    level = one(*shards[0])
    for cut in shards[1:]:
        level = level * one(*cut)
    return level


def noise(stream_key, shape, deviation, bound, cuts=(), kind=jnp.bfloat16):
    factor_of = levels(stream_key, shape, cuts, -0.22, 0.18) if cuts else 1.0
    drawn = jax.random.normal(stream_key, shape, jnp.float32) * deviation * factor_of
    return jnp.minimum(jnp.maximum(drawn, -bound), bound).astype(kind)


def setup_inputs(seed: int = 0) -> dict:
    streams_of = jax.random.split(jax.random.key(seed), 13)
    inputs = noise(streams_of[0], (MB, SEQ_FS, LENGTH, D), 1.0, 6.0, ((1, 4), (2, 4)))
    cotangent = noise(streams_of[1], (MB, SEQ_FS, LENGTH, D), 1.0, 6.0, ((1, 4), (2, 4)))
    segments = draw_segments(jax.random.fold_in(streams_of[12], 71), 0)
    w_query = noise(streams_of[3], (2, D, QW), D ** -0.5, 0.1875, ((0, 2), (1, 16)))
    w_key = noise(streams_of[4], (2, D, KW), D ** -0.5, 0.1875, ((0, 2), (1, 16)))
    w_value = noise(streams_of[5], (2, D, KW), D ** -0.5, 0.1875, ((0, 2), (1, 16)))
    w_out = noise(streams_of[6], (2, QW, D), (QW // 16) ** -0.5, 0.75, ((0, 2), (2, 16)))
    w_gate = noise(streams_of[7], (2, D, FF), D ** -0.5, 0.1875, ((0, 2), (1, 16)))
    w_up = noise(streams_of[8], (2, D, FF), D ** -0.5, 0.1875, ((0, 2), (1, 16)))
    w_down = noise(streams_of[9], (2, FF, D), FF ** -0.5, 0.109375, ((0, 2), (2, 16)))
    norm_attn = jnp.clip(1.0 + 0.15 * jax.random.normal(streams_of[10], (2, D), jnp.float32), 0.25, 1.75).astype(jnp.bfloat16)
    norm_mlp = jnp.clip(1.0 + 0.15 * jax.random.normal(streams_of[11], (2, D), jnp.float32), 0.25, 1.75).astype(jnp.bfloat16)
    return {"inputs": inputs, "cotangent": cotangent, "segments": segments, "w_query": w_query, "w_key": w_key, "w_value": w_value, "w_out": w_out, "w_gate": w_gate, "w_up": w_up, "w_down": w_down, "norm_attn": norm_attn, "norm_mlp": norm_mlp}


epsilon = 1e-05
rope_base = 10000.0
neg_large = -1e+30

@jax.custom_vjp
def low(v):
    return lax.optimization_barrier(v.astype(jnp.bfloat16)).astype(jnp.float32)

@jax.custom_vjp
def low_back(v):
    return v

def low_keep(v):
    return (low(v), None)

def low_pass(kept, grad):
    return (grad,)

def back_keep(v):
    return (v, None)

def back_low(kept, grad):
    return (low(grad),)
low.defvjp(low_keep, low_pass)
low_back.defvjp(back_keep, back_low)

def rope_turn(value_rows, positions, direction):
    head_count = value_rows.shape[-1] // HEAD_SIZE
    pieces = value_rows.reshape(value_rows.shape[:-1] + (head_count, HEAD_SIZE))
    half_dim = HEAD_SIZE // 2
    frequency = rope_base ** (-2.0 * jnp.arange(half_dim).astype(value_rows.dtype) / HEAD_SIZE)
    angles = positions.astype(value_rows.dtype)[:, None] * frequency[None, :]
    cosine = jnp.cos(angles)[:, None, :]
    sine_part = direction * jnp.sin(angles)[:, None, :]
    first_half = pieces[..., :half_dim]
    second_half = pieces[..., half_dim:]
    turned = jnp.concatenate([first_half * cosine - second_half * sine_part, second_half * cosine + first_half * sine_part], axis=-1)
    return turned.reshape(value_rows.shape)

def rms_scale(value_rows, gain):
    return value_rows * lax.rsqrt(lax.optimization_barrier(jnp.mean(value_rows * value_rows, axis=-1, keepdims=True)) + epsilon) * gain

def matmul(left, right):
    return jnp.dot(left, right, precision=lax.Precision.HIGHEST)

def attention(query_rows, key_rows, value_rows, seg_ids):
    span_length = query_rows.shape[0]
    block_length = min(512, span_length)
    block_count = span_length // block_length
    query_groups = query_rows.shape[1] // key_rows.shape[1]
    key_head_rows = key_rows.reshape(span_length, KEY_VALUE_HEADS, HEAD_SIZE)
    value_head_rows = value_rows.reshape(span_length, KEY_VALUE_HEADS, HEAD_SIZE)
    positions = jnp.arange(span_length, dtype=jnp.int32)

    def one_block(block_index):
        start_offset = (block_index * block_length).astype(jnp.int32)
        query_block = lax.dynamic_slice_in_dim(query_rows, start_offset, block_length, 0).reshape(block_length, KEY_VALUE_HEADS, query_groups, HEAD_SIZE)
        q_pos = start_offset + jnp.arange(block_length, dtype=jnp.int32)
        q_seg = lax.dynamic_slice_in_dim(seg_ids, start_offset, block_length, 0)
        raw_scores = jnp.einsum('cngd,pnd->ngcp', query_block, key_head_rows, precision=lax.Precision.HIGHEST) * 0.125
        scores = low_back(raw_scores)
        same_doc = seg_ids[None, :] == q_seg[:, None]
        causal = positions[None, :] <= q_pos[:, None]
        diagonal = positions[None, :] == q_pos[:, None]
        allowed = same_doc & causal & ((q_seg[:, None] != 0) | diagonal)
        scores = jnp.where(allowed[None, None], scores, neg_large)
        probs = low(jax.nn.softmax(scores, axis=-1))
        result = jnp.einsum('ngcp,pnd->cngd', probs, value_head_rows, precision=lax.Precision.HIGHEST)
        return result.reshape(block_length, -1)
    blocks = lax.map(jax.checkpoint(one_block), jnp.arange(block_count, dtype=jnp.int32))
    return blocks.reshape(span_length, -1)

def layer(x_float, params, seg_ids):
    q_weight, k_weight, v_weight, o_weight, g_weight, u_weight, d_weight, gain_one, gain_two = params
    span_length = x_float.shape[0]
    positions = jnp.arange(span_length, dtype=jnp.int32)
    normed = low(rms_scale(x_float, gain_one))
    query_rows = low(rope_turn(low_back(matmul(normed, q_weight)), positions, 1.0))
    key_rows = low(rope_turn(low_back(matmul(normed, k_weight)), positions, 1.0))
    value_rows = low(low_back(matmul(normed, v_weight)))
    attended = low(low_back(attention(query_rows, key_rows, value_rows, seg_ids)))
    mixed = x_float + low_back(matmul(attended, o_weight))
    normed_two = low(rms_scale(mixed, gain_two))
    gate = low_back(matmul(normed_two, g_weight))
    up_val = low_back(matmul(normed_two, u_weight))
    hidden = low(jax.nn.silu(gate) * up_val)
    return mixed + low_back(matmul(hidden, d_weight))

def reference(inputs, cotangent, segments, w_query, w_key, w_value, w_out, w_gate, w_up, w_down, norm_attn, norm_mlp):
    flat_x = inputs.astype(jnp.float32).reshape(-1, LENGTH, D)
    flat_seg = segments.reshape(-1, LENGTH).astype(jnp.int32)
    probe = jnp.zeros_like(flat_x)
    weights = tuple((item.astype(jnp.float32) for item in (w_query, w_key, w_value, w_out, w_gate, w_up, w_down, norm_attn, norm_mlp)))

    def forward(x_all, probe_all, weight_all):
        first_layer = tuple((item[0] for item in weight_all))
        second_layer = tuple((item[1] for item in weight_all))

        def per_seq(carry, item):
            x_one, probe_one, seg_one = item
            between = low(low_back(layer(x_one, first_layer, seg_one))) + probe_one
            return (carry, (between, layer(between, second_layer, seg_one)))
        _, (between_all, final_all) = lax.scan(jax.checkpoint(per_seq), jnp.zeros((), jnp.float32), (x_all, probe_all, flat_seg))
        return (between_all, final_all)
    (between_all, final_all), pullback = jax.vjp(forward, flat_x, probe, weights)
    grad_x, grad_between, grad_w = pullback((jnp.zeros_like(between_all), cotangent.astype(jnp.float32).reshape(final_all.shape)))
    out_shape = (MB, SEQ_FS, LENGTH, D)
    layer_out = jnp.stack([between_all.reshape(out_shape), final_all.reshape(out_shape)]).astype(jnp.bfloat16)
    input_grad = jnp.stack([grad_x.reshape(out_shape), grad_between.reshape(out_shape)]).astype(jnp.bfloat16)
    return (layer_out, input_grad, grad_w[0], grad_w[1], grad_w[2], grad_w[3], grad_w[4], grad_w[5], grad_w[6], grad_w[7], grad_w[8])
```

```python
import functools

import jax
import jax.numpy as jnp
from jax import lax
from jax.experimental import pallas as pl
from jax.experimental.pallas import tpu as pltpu
from jax.sharding import PartitionSpec as P

HEAD = 64
PAIR = 2 * HEAD
EPSILON = 1e-05
ROPE_BASE = 10000.0
NEG = -1e30
GAIN_COLS = 64
LARGE = pl.CostEstimate(flops=1 << 34, bytes_accessed=1024, transcendentals=0)
SMALL = pl.CostEstimate(flops=1024, bytes_accessed=1024, transcendentals=0)
BF16 = jnp.bfloat16
F32 = jnp.float32
NT = (((1,), (1,)), ((), ()))
TN = (((0,), (0,)), ((), ()))
NN = (((1,), (0,)), ((), ()))


def dot(left, right, dims=NN):
    return lax.dot_general(left, right, dims, preferred_element_type=F32)


def swap_halves(value):
    lane = lax.broadcasted_iota(jnp.int32, value.shape, 1)
    ahead = pltpu.roll(value, PAIR - HEAD // 2, 1)
    behind = pltpu.roll(value, HEAD // 2, 1)
    return jnp.where(lane % HEAD < HEAD // 2, ahead, behind)


def rope_tables(positions):
    half = HEAD // 2
    frequency = ROPE_BASE ** (-2.0 * jnp.arange(half, dtype=F32) / HEAD)
    angles = positions.astype(F32)[:, None] * frequency[None, :]
    cosine, sine = jnp.cos(angles), jnp.sin(angles)
    return (
        jnp.concatenate([cosine] * 4, axis=1),
        jnp.concatenate([-sine, sine, -sine, sine], axis=1),
    )


def head_slots(ref, kinds, cos_ref, sin_ref, places, block):
    rows = ref.shape[0]

    def step(i, carry):
        at = pl.ds(pl.multiple_of(i * block, block), block)
        cosine, sine = cos_ref[at, :], sin_ref[at, :]
        for low in range(0, len(kinds), 2):
            pair = range(low, min(low + 2, len(kinds)))
            raw = ref[at, low * HEAD : (pair[-1] + 1) * HEAD].astype(F32)
            if len(pair) == 1:
                raw = jnp.concatenate([raw, raw], axis=1)
            turned = raw
            if any(kinds[slot] != "v" for slot in pair):
                turned = raw * cosine + swap_halves(raw) * sine
            for slot in pair:
                kind = kinds[slot]
                value = raw if kind == "v" else turned
                value = value[:, (slot - low) * HEAD : (slot - low + 1) * HEAD]
                if kind == "q":
                    value = value * 0.125
                dest, index = places[slot]
                dest[index, at, :] = value.astype(BF16)
        return carry

    lax.fori_loop(0, rows // block, step, 0)


def forward_kernel(hq, hk, same, *refs):
    if same:
        q_ref, cosq, sinq, segq, posq, segk, o_ref, qh, kvh, lse_ref, bias, oh, lsec = refs
    else:
        q_ref, kv_ref, cosq, sinq, cosk, sink, segq, posq, segk = refs[:9]
        o_ref, qh, kvh, lse_ref, bias, oh, lsec = refs[9:]
    rows, keys = bias.shape
    block = min(256, rows)
    count = rows // block
    group = hq // hk
    q_kinds, q_places = ["q"] * hq, [(qh, i) for i in range(hq)]
    kv_kinds = ["k"] * hk + ["v"] * hk
    kv_places = [(kvh, i) for i in range(2 * hk)]
    if same:
        head_slots(q_ref, q_kinds + kv_kinds, cosq, sinq, q_places + kv_places, block)
    else:
        head_slots(q_ref, q_kinds, cosq, sinq, q_places, block)
        head_slots(kv_ref, kv_kinds, cosk, sink, kv_places, block)
    for i in range(count):
        at = slice(i * block, (i + 1) * block)
        width = (i + 1) * block if same else keys
        seg_q, pos_q = segq[at, :], posq[at, :]
        seg_k = segk[:, :width]
        pos_k = lax.broadcasted_iota(jnp.int32, (block, width), 1)
        seen = (seg_q == seg_k) & (pos_k <= pos_q) & ((seg_q != 0) | (pos_k == pos_q))
        bias[at, :width] = jnp.where(seen, 0.0, NEG)

    def one_head(h, carry):
        g = lax.div(h, group)
        for i in range(count):
            at = slice(i * block, (i + 1) * block)
            width = (i + 1) * block if same else keys
            scores = dot(qh[h, at, :], kvh[g, :width, :], NT) + bias[at, :width]
            top = jnp.max(scores, axis=1, keepdims=True)
            probs = jnp.exp(scores - top)
            mass = jnp.sum(probs, axis=1, keepdims=True)
            summed = dot(probs.astype(BF16), kvh[hk + g, :width, :])
            oh[h, at, :] = summed / mass
            lane = lax.broadcasted_iota(jnp.int32, (block, 128), 1)
            lsec[at, :] = jnp.where(lane == h, top + jnp.log(mass), lsec[at, :])
        return carry

    lsec[...] = jnp.zeros_like(lsec)
    lax.fori_loop(0, hq, one_head, 0)
    for low in range(0, hq, 2):
        pair = [oh[slot] for slot in range(low, min(low + 2, hq))]
        value = jnp.concatenate(pair, axis=1) if len(pair) == 2 else pair[0]
        o_ref[:, low * HEAD : low * HEAD + value.shape[1]] = value.astype(BF16)
    lse_ref[...] = jnp.transpose(lsec[...])[: lse_ref.shape[0], :]


def unturn(heads, ref, cosine, sine, kinds, block):
    rows = ref.shape[0]

    def step(i, carry):
        at = pl.ds(pl.multiple_of(i * block, block), block)
        cos_part, sin_part = cosine[at, :], sine[at, :]
        for low in range(0, len(kinds), 2):
            pair = range(low, min(low + 2, len(kinds)))
            pieces = [heads[slot][0][heads[slot][1], at, :] for slot in pair]
            raw = jnp.concatenate(pieces if len(pieces) == 2 else pieces * 2, axis=1)
            if kinds[low] != "v":
                turned = raw * cos_part - swap_halves(raw) * sin_part
                if kinds[pair[-1]] == "v":
                    lane = lax.broadcasted_iota(jnp.int32, raw.shape, 1)
                    turned = jnp.where(lane < HEAD, turned, raw)
                raw = turned
            width = len(pieces) * HEAD
            ref[at, low * HEAD : low * HEAD + width] = raw[:, :width].astype(ref.dtype)
        return carry

    lax.fori_loop(0, rows // block, step, 0)


def backward_kernel(hq, hk, same, *refs):
    if same:
        qh, kvh, do_ref, o_ref, lse_ref, cosq, sinq, segq, posq, segk, w_ref = refs[:11]
        dqkv_ref, own_ref, bias, doh, delta, dqs, dks, dvs = refs[11:]
    else:
        qh, kvh, do_ref, o_ref, lse_ref = refs[:5]
        cosq, sinq, cosk, sink, segq, posq, segk = refs[5:12]
        dq_ref, dkv_ref, bias, doh, delta, dqs, dks, dvs = refs[12:]
    keys, rows = bias.shape
    block = min(256, rows)
    count = rows // block
    group = hq // hk
    for i in range(count):
        at = slice(i * block, (i + 1) * block)
        width = (i + 1) * block if same else keys
        seg_q, pos_q = segq[:, at], posq[:, at]
        seg_k = segk[:width, :]
        pos_k = lax.broadcasted_iota(jnp.int32, (width, block), 0)
        seen = (seg_q == seg_k) & (pos_k <= pos_q) & ((seg_q != 0) | (pos_k == pos_q))
        bias[:width, at] = jnp.where(seen, 0.0, NEG)
    for h in range(hq):
        doh[h] = do_ref[:, h * HEAD : (h + 1) * HEAD]
    wide = do_ref.shape[1]
    marks = lax.broadcasted_iota(jnp.int32, (delta.shape[0], wide), 1) // HEAD
    marks = (marks == lax.broadcasted_iota(jnp.int32, marks.shape, 0)).astype(F32)
    products = do_ref[...].astype(F32) * o_ref[...].astype(F32)
    delta[...] = lax.dot_general(
        marks, products, NT, precision=lax.Precision.HIGHEST, preferred_element_type=F32
    )

    def one_group(g, carry):
        dks[g] = jnp.zeros(dks.shape[1:], F32)
        dvs[g] = jnp.zeros(dvs.shape[1:], F32)

        def one_head(j, inner):
            h = g * group + j
            for i in range(count):
                at = slice(i * block, (i + 1) * block)
                width = (i + 1) * block if same else keys
                query, grad = qh[h, at, :], doh[h, at, :]
                key, value = kvh[g, :width, :], kvh[hk + g, :width, :]
                scores = dot(key, query, NT) + bias[:width, at]
                probs = jnp.exp(scores - lse_ref[pl.ds(h, 1), at])
                grad_probs = dot(value, grad, NT)
                grad_scores = (probs * (grad_probs - delta[pl.ds(h, 1), at])).astype(BF16)
                dvs[g, :width, :] += dot(probs.astype(BF16), grad)
                dks[g, :width, :] += dot(grad_scores, query)
                dqs[h, at, :] = dot(grad_scores, key, TN) * 0.125
            return inner

        lax.fori_loop(0, group, one_head, 0)
        return carry

    lax.fori_loop(0, hk, one_group, 0)
    q_heads = [(dqs, i) for i in range(hq)]
    kv_heads = [(dks, i) for i in range(hk)] + [(dvs, i) for i in range(hk)]
    kinds = ["k"] * hk + ["v"] * hk
    if same:
        unturn(q_heads + kv_heads, dqkv_ref, cosq, sinq, ["q"] * hq + kinds, block)

        def project(i, carry):
            at = pl.ds(pl.multiple_of(i * block, block), block)
            weight = w_ref[:, : dqkv_ref.shape[1]]
            own_ref[at, :] = dot(dqkv_ref[at, :], weight, NT).astype(BF16)
            return carry

        lax.fori_loop(0, count, project, 0)
    else:
        unturn(q_heads, dq_ref, cosq, sinq, ["q"] * hq, block)
        unturn(kv_heads, dkv_ref, cosk, sink, kinds, block)


def whole(value):
    zeros = (0,) * len(value.shape)
    return pl.BlockSpec(value.shape, lambda i: zeros, pipeline_mode=pl.Buffered(1))


def in_hbm(arrays):
    return [pltpu.with_memory_space_constraint(value, pltpu.HBM) for value in arrays]


def attention_forward(qkv, plan):
    hq, hk, same = plan["hq"], plan["hk"], plan["same"]
    rows = qkv.shape[0]
    if same:
        keys = rows
        args = [qkv, *plan["tables_q"], plan["seg_q_col"], plan["pos_q_col"], plan["seg_k_row"]]
    else:
        kv_all = plan["gather"](qkv[:, hq * HEAD :])
        keys = kv_all.shape[0]
        args = [qkv[:, : hq * HEAD], kv_all, *plan["tables_q"], *plan["tables_k"]]
        args += [plan["seg_q_col"], plan["pos_q_col"], plan["seg_k_row"]]
    lines = -(-hq // 8) * 8
    out_shape = (
        pltpu.HBM((rows, hq * HEAD), BF16),
        pltpu.HBM((hq, rows, HEAD), BF16),
        pltpu.HBM((2 * hk, keys, HEAD), BF16),
        pltpu.HBM((lines, rows), F32),
    )
    return pl.pallas_call(
        functools.partial(forward_kernel, hq, hk, same),
        out_shape=out_shape,
        grid=(1,),
        in_specs=[whole(value) for value in args],
        out_specs=[whole(value) for value in out_shape],
        scratch_shapes=[
            pltpu.VMEM((rows, keys), F32),
            pltpu.VMEM((hq, rows, HEAD), F32),
            pltpu.VMEM((rows, 128), F32),
        ],
        compiler_params=pltpu.CompilerParams(vmem_limit_bytes=30 * 2**20),
        cost_estimate=SMALL,
    )(*in_hbm(args))


def attention_backward(kept, d_out, w_attn, qkv_cols, plan):
    hq, hk, same = plan["hq"], plan["hk"], plan["same"]
    out, qh, kvh, lse = kept
    rows, keys = out.shape[0], kvh.shape[1]
    args = [qh, kvh, d_out, out, lse, *plan["tables_q"]]
    if not same:
        args += list(plan["tables_k"])
    args += [plan["seg_q_row"], plan["pos_q_row"], plan["seg_k_col"]]
    if same:
        args.append(w_attn)
        out_shape = (
            pltpu.HBM((rows, qkv_cols), BF16),
            jax.ShapeDtypeStruct((rows, w_attn.shape[0]), BF16),
        )
    else:
        out_shape = (
            jax.ShapeDtypeStruct((rows, hq * HEAD), BF16),
            jax.ShapeDtypeStruct((keys, 2 * hk * HEAD), F32),
        )
    result = pl.pallas_call(
        functools.partial(backward_kernel, hq, hk, same),
        out_shape=out_shape,
        grid=(1,),
        in_specs=[whole(value) for value in args],
        out_specs=[whole(value) for value in out_shape],
        scratch_shapes=[
            pltpu.VMEM((keys, rows), F32),
            pltpu.VMEM((hq, rows, HEAD), BF16),
            pltpu.VMEM((lse.shape[0], rows), F32),
            pltpu.VMEM((hq, rows, HEAD), F32),
            pltpu.VMEM((hk, keys, HEAD), F32),
            pltpu.VMEM((hk, keys, HEAD), F32),
        ],
        compiler_params=pltpu.CompilerParams(vmem_limit_bytes=40 * 2**20),
        cost_estimate=SMALL,
    )(*in_hbm(args))
    if same:
        return result
    d_kv = plan["scatter"](result[1]).astype(BF16)
    d_qkv = jnp.concatenate([result[0], d_kv], axis=1)
    return d_qkv, dot(d_qkv, w_attn[:, :qkv_cols], NT).astype(BF16)


def other_core(value):
    return lax.ppermute(value, "section", [(0, 1), (1, 0)])


def place(buffer, block, index):
    return lax.dynamic_update_index_in_dim(buffer, block, index, 0)


def pick(blocks, index):
    return lax.dynamic_index_in_dim(blocks, index, 0, False)


def flip(value, axis, step, group=None):
    size = group or lax.axis_size(axis)
    pairs = [(i, i - i % size + (i % size ^ step)) for i in range(lax.axis_size(axis))]
    return lax.ppermute(value, axis, pairs)


class Return:
    def __init__(self, first, second, places, core, parts, pinned=False):
        self.places, self.core, self.parts = places, core, parts
        self.received = in_hbm if pinned else list
        self.blocks = [v.reshape(2 * parts, -1, v.shape[1]) for v in (first, second)]
        to_x, to_y = self.packed(((1, 0), (3, 0)), ((2, 1), (3, 1)))
        self.near = [flip(to_x, "seq", 1, parts), flip(to_y, "seq", 2, parts)]

    def packed(self, *sends):
        rows, width = self.blocks[0].shape[1:]
        half = rows // 2

        def body(places_ref, core_ref, *refs):
            source, outs = iter(refs[: len(ins)]), refs[len(ins) :]
            for send, out in zip(sends, outs):
                for i, block in enumerate(send):
                    if isinstance(block[0], int):
                        first, second = next(source), next(source)
                        out[i] = jnp.where(core_ref[0] == 0, first[0], second[0])
                    else:
                        out[i] = next(source)[0]

        ins, in_specs = [], []
        for send in sends:
            for place_index, part in send:
                if isinstance(place_index, int):
                    ins += self.blocks

                    def index(i, o, c, place_index=place_index, part=part):
                        return (2 * o[place_index] + part, i, 0)

                    in_specs += [pl.BlockSpec((1, half, width), index)] * 2
                else:
                    ins += self.received([place_index])

                    def index(i, o, c, part=part):
                        return (part, i, 0)

                    in_specs.append(pl.BlockSpec((1, half, width), index))
        return pl.pallas_call(
            body,
            out_shape=[jax.ShapeDtypeStruct((len(send), rows, width), BF16) for send in sends],
            grid_spec=pltpu.PrefetchScalarGridSpec(
                num_scalar_prefetch=2,
                grid=(2,),
                in_specs=in_specs,
                out_specs=[
                    pl.BlockSpec((len(send), half, width), lambda i, o, c: (0, i, 0))
                    for send in sends
                ],
            ),
            compiler_params=pltpu.CompilerParams(vmem_limit_bytes=8 * 2**20),
            cost_estimate=SMALL,
        )(self.places, self.core, *ins)

    def onward(self):
        near_x, near_y = self.near
        to_y, to_x = self.packed(((2, 0), (near_x, 1)), ((1, 1), (near_y, 1)))
        self.far = [flip(to_y, "seq", 2, self.parts), flip(to_x, "seq", 1, self.parts)]

    def placed(self):
        near_x, near_y = self.near
        far_y, far_x = self.far
        rows, width = self.blocks[0].shape[1:]
        half, parts = rows // 2, self.parts

        def body(places_ref, core_ref, first_a, second_a, first_b, second_b, nx, ny, fy, fx, out):
            mine = core_ref[0] == 0
            out[2 * places_ref[0]] = jnp.where(mine, first_a[0], second_a[0])
            out[2 * places_ref[0] + 1] = jnp.where(mine, first_b[0], second_b[0])
            out[2 * places_ref[1]] = nx[0]
            out[2 * places_ref[1] + 1] = fx[0]
            out[2 * places_ref[2]] = fy[0]
            out[2 * places_ref[2] + 1] = ny[0]
            out[2 * places_ref[3]] = fy[1]
            out[2 * places_ref[3] + 1] = fx[1]

        def own(part):
            return pl.BlockSpec((1, half, width), lambda i, o, c: (2 * o[0] + part, i, 0))

        def spec(count):
            return pl.BlockSpec((count, half, width), lambda i, o, c: (0, i, 0))

        result = pl.pallas_call(
            body,
            out_shape=jax.ShapeDtypeStruct((2 * parts, rows, width), BF16),
            grid_spec=pltpu.PrefetchScalarGridSpec(
                num_scalar_prefetch=2,
                grid=(2,),
                in_specs=[own(0), own(0), own(1), own(1), spec(1), spec(1), spec(2), spec(2)],
                out_specs=spec(2 * parts),
            ),
            compiler_params=pltpu.CompilerParams(vmem_limit_bytes=12 * 2**20),
            cost_estimate=SMALL,
        )(
            self.places,
            self.core,
            *self.blocks,
            *self.blocks,
            *self.received((near_x, near_y, far_y, far_x)),
        )
        return result.reshape(parts, 2 * rows, width)


ANY = pl.BlockSpec(memory_space=pl.ANY)
VMEM = pl.BlockSpec(memory_space=pltpu.VMEM)


def shapes_of(arrays, pinned=()):
    kinds = [jax.ShapeDtypeStruct] * len(arrays) + [pltpu.HBM] * len(pinned)
    return [kind(v.shape, v.dtype) for kind, v in zip(kinds, (*arrays, *pinned))]


def hold(*arrays, pinned=()):
    def body(*refs):
        pass

    count = len(arrays) + len(pinned)
    return pl.pallas_call(
        body,
        out_shape=shapes_of(arrays, pinned),
        in_specs=[ANY] * count,
        out_specs=[ANY] * count,
        input_output_aliases={i: i for i in range(count)},
        compiler_params=pltpu.CompilerParams(vmem_limit_bytes=2**20),
        cost_estimate=SMALL,
    )(*arrays, *in_hbm(pinned))


def assemble(order, column, by_x, by_y, far_low, far_high, held, pinned):
    def body(order_ref, col, bx, by, low, high, *refs):
        out = refs[count]
        for i, source in enumerate((col, bx, by)):
            out[pl.ds(2 * order_ref[i], 2)] = source[...]
        out[2 * order_ref[3]] = low[...]
        out[2 * order_ref[3] + 1] = high[...]

    half, cols = column.shape[1:]
    rows = half // 3
    count = len(held) + len(pinned)

    def spec(count):
        return pl.BlockSpec((count, rows, cols), lambda i, o: (0, i, 0))

    single = pl.BlockSpec((rows, cols), lambda i, o: (i, 0))
    result = pl.pallas_call(
        body,
        out_shape=[jax.ShapeDtypeStruct((8, half, cols), column.dtype)]
        + shapes_of(held, pinned),
        grid_spec=pltpu.PrefetchScalarGridSpec(
            num_scalar_prefetch=1,
            grid=(3,),
            in_specs=[spec(2)] * 3 + [single] * 2 + [ANY] * count,
            out_specs=[spec(8)] + [ANY] * count,
        ),
        input_output_aliases={6 + i: 1 + i for i in range(count)},
        compiler_params=pltpu.CompilerParams(vmem_limit_bytes=16 * 2**20),
        cost_estimate=SMALL,
    )(order, column, by_x, by_y, far_low, far_high, *held, *in_hbm(pinned))
    return (result[0].reshape(8 * half, cols), *result[1:])


def gradient_chunk(d_qkv, attended, columns, scales):
    tokens, width = columns[0].shape
    first, last = d_qkv.shape[1], attended.shape[1]
    offset = first + GAIN_COLS
    rows = width // 3

    def body(d_ref, o_ref, a_ref, m_ref, own_a, val_a, own_b, val_b, r_a, r_b, out_ref):
        out_ref[:, :first] = dot(a_ref[...], d_ref[...], TN).astype(BF16)
        lane = lax.broadcasted_iota(jnp.int32, (tokens, GAIN_COLS), 1)
        gains = jnp.zeros((rows, GAIN_COLS), F32)
        for i, (own, val, r) in enumerate(((own_a, val_a, r_a), (own_b, val_b, r_b))):
            product = own[...].astype(F32) * val[...].astype(F32) * r[...]
            unit = jnp.where(lane == i, 1.0, 0.0).astype(BF16)
            gains += dot(product.astype(BF16), unit, TN)
        out_ref[:, first:offset] = gains.astype(BF16)
        out_ref[:, offset:] = dot(m_ref[...], o_ref[...], TN).astype(BF16)

    def part(cols):
        return pl.BlockSpec((tokens, cols), lambda i: (0, 0))

    block = pl.BlockSpec((tokens, rows), lambda i: (0, i))
    return pl.pallas_call(
        body,
        out_shape=pltpu.HBM((width, offset + last), BF16),
        grid=(3,),
        in_specs=[part(first), part(last)] + [block] * 6 + [part(1)] * 2,
        out_specs=pl.BlockSpec((rows, offset + last), lambda i: (i, 0)),
        compiler_params=pltpu.CompilerParams(vmem_limit_bytes=36 * 2**20),
        cost_estimate=LARGE,
    )(*in_hbm((d_qkv, attended, *columns, *scales)))


def norm_back(own, other, value, scale, gain, added, weight=None):
    tokens, width = own.shape
    rows = min(256, tokens)
    low, cols = (weight[1], weight[0].shape[1] - weight[1]) if weight else (0, 0)

    def body(own_ref, other_ref, value_ref, scale_ref, gain_ref, added_ref, *refs):
        grad = (own_ref[...].astype(F32) + other_ref[...].astype(F32)) * gain_ref[...]
        val, r = value_ref[...].astype(F32), scale_ref[...]
        mean = jnp.sum(grad * val, axis=1, keepdims=True) * (1.0 / width)
        result = added_ref[...].astype(F32) + r * grad - val * (r * r * r * mean)
        result = result.astype(BF16)
        refs[-2 if weight else -1][...] = result
        if weight:
            refs[-1][...] = dot(result, refs[0][:, low:]).astype(BF16)

    block = pl.BlockSpec((rows, width), lambda i: (i, 0))
    scales = pl.BlockSpec((rows, 1), lambda i: (i, 0))
    ins = [own, other, value, scale, gain[None, :], added]
    in_specs = [block, block, block, scales, pl.BlockSpec((1, width), lambda i: (0, 0)), block]
    out_shape, out_specs = [pltpu.HBM((tokens, width), BF16)], [block]
    if weight:
        ins.append(weight[0])
        in_specs.append(pl.BlockSpec(weight[0].shape, lambda i: (0, 0)))
        out_shape.append(pltpu.HBM((tokens, cols), BF16))
        out_specs.append(pl.BlockSpec((rows, cols), lambda i: (i, 0)))
    return pl.pallas_call(
        body,
        out_shape=out_shape,
        grid=(tokens // rows,),
        in_specs=in_specs,
        out_specs=out_specs,
        compiler_params=pltpu.CompilerParams(vmem_limit_bytes=24 * 2**20),
        cost_estimate=SMALL,
    )(*in_hbm(ins))


def row_specs(tokens, rows, widths):
    return [pl.BlockSpec((rows, width), lambda i: (i, 0)) for width in widths]


def mlp_forward(normed, weight):
    tokens, width = normed.shape
    rows, half_ff = min(256, tokens), weight.shape[1] // 3

    def body(b_ref, w_ref, gate_ref, up_ref, hidden_ref, part_ref):
        gate = dot(b_ref[...], w_ref[:, :half_ff])
        up = dot(b_ref[...], w_ref[:, half_ff : 2 * half_ff])
        hidden = (gate * jax.nn.sigmoid(gate) * up).astype(BF16)
        gate_ref[...] = gate.astype(BF16)
        up_ref[...] = up.astype(BF16)
        hidden_ref[...] = hidden
        part_ref[...] = dot(hidden, w_ref[:, 2 * half_ff :], NT).astype(BF16)

    widths = (half_ff, half_ff, half_ff, width)
    return pl.pallas_call(
        body,
        out_shape=[pltpu.HBM((tokens, w), BF16) for w in widths[:3]]
        + [jax.ShapeDtypeStruct((tokens, width), BF16)],
        grid=(tokens // rows,),
        in_specs=row_specs(tokens, rows, (width,)) + [VMEM],
        out_specs=row_specs(tokens, rows, widths),
        compiler_params=pltpu.CompilerParams(vmem_limit_bytes=22 * 2**20),
        cost_estimate=SMALL,
    )(normed, weight)


def mlp_backward(grad, gate, up, weight):
    tokens, width = grad.shape
    rows, half_ff = min(256, tokens), weight.shape[1] // 3

    def body(g_ref, gate_ref, up_ref, w_ref, d_gu_ref, part_ref):
        d_hidden = dot(g_ref[...], w_ref[:, 2 * half_ff :])
        z = gate_ref[...].astype(F32)
        sigma = jax.nn.sigmoid(z)
        d_gate = d_hidden * up_ref[...].astype(F32) * sigma * (1.0 + z * (1.0 - sigma))
        d_gate = d_gate.astype(BF16)
        d_up = (d_hidden * z * sigma).astype(BF16)
        d_gu_ref[:, :half_ff] = d_gate
        d_gu_ref[:, half_ff:] = d_up
        part = dot(d_gate, w_ref[:, :half_ff], NT)
        part += dot(d_up, w_ref[:, half_ff : 2 * half_ff], NT)
        part_ref[...] = part.astype(BF16)

    widths = (2 * half_ff, width)
    return pl.pallas_call(
        body,
        out_shape=[
            pltpu.HBM((tokens, widths[0]), BF16),
            jax.ShapeDtypeStruct((tokens, width), BF16),
        ],
        grid=(tokens // rows,),
        in_specs=row_specs(tokens, rows, (width, half_ff, half_ff)) + [VMEM],
        out_specs=row_specs(tokens, rows, widths),
        compiler_params=pltpu.CompilerParams(vmem_limit_bytes=22 * 2**20),
        cost_estimate=SMALL,
    )(*in_hbm((grad, gate, up)), weight)


def sum_step(order, add, add_pinned, pack, last, held, pinned):
    ins, in_specs, out_shape, out_specs = [], [], [], []

    def block(array, which, part, pinned=False):
        rows = array.shape[1] // 3
        (array,) = in_hbm([array]) if pinned else [array]
        spec = pl.BlockSpec((1, rows, array.shape[2]), lambda i, o: (2 * o[which] + part, i, 0))
        ins.append(array)
        in_specs.append(spec)

    def pair(half, cols):
        return pl.BlockSpec((2, half // 3, cols), lambda i, o: (0, i, 0))

    def single(half, cols):
        return pl.BlockSpec((half // 3, cols), lambda i, o: (i, 0))

    def size(terms):
        return terms[0].shape[1], sum(value.shape[2] for value in terms)

    def places(terms):
        low = 0
        for value in terms:
            yield slice(low, low + value.shape[2])
            low += value.shape[2]

    if add is not None:
        terms, got_x, got_y = add
        half, cols = size(terms)
        for value in terms:
            for which, part in ((0, 0), (0, 1), (2, 0), (1, 1)):
                block(value, which, part, add_pinned)
        ins += [got_x, got_y]
        in_specs += [pair(half, cols)] * 2
        out_shape += [jax.ShapeDtypeStruct((half, cols), BF16)] * 2
        out_shape += [jax.ShapeDtypeStruct((2, half, cols), BF16)]
        out_specs += [single(half, cols), single(half, cols), pair(half, cols)]
    if pack is not None:
        half, cols = size(pack)
        for value in pack:
            for which, part in ((1, 0), (3, 0), (2, 1), (3, 1)):
                block(value, which, part)
        out_shape += [jax.ShapeDtypeStruct((2, half, cols), BF16)] * 2
        out_specs += [pair(half, cols)] * 2
    if last:
        for chunk in last:
            half, cols = chunk[1].shape
            ins += list(chunk)
            in_specs += [pair(half, cols), single(half, cols), single(half, cols)]
        half, cols = size([chunk[0] for chunk in last])
        out_shape += [jax.ShapeDtypeStruct((2, half, cols), BF16)]
        out_specs += [pair(half, cols)]

    def plus(left, right):
        return (left.astype(F32) + right.astype(F32)).astype(BF16)

    count = len(held) + len(pinned)

    def body(order_ref, *refs):
        source = iter(refs[: len(ins)])
        target = iter(refs[len(ins) + count :])
        if add is not None:
            blocks = [[next(source) for _ in range(4)] for _ in add[0]]
            gx, gy = next(source), next(source)
            to_y, to_x, kept = (next(target) for _ in range(3))
            for (own_a, own_b, on_a, on_b), at in zip(blocks, places(add[0])):
                to_y[:, at] = plus(on_a[0], gx[1, :, at])
                to_x[:, at] = plus(on_b[0], gy[1, :, at])
                kept[0, :, at] = plus(own_a[0], gx[0, :, at])
                kept[1, :, at] = plus(own_b[0], gy[0, :, at])
        if pack is not None:
            outs = next(target), next(target)
            for at in places(pack):
                for out in outs:
                    for i in range(2):
                        out[i, :, at] = next(source)[0]
        if last:
            out = next(target)
            for at in places([chunk[0] for chunk in last]):
                kept, from_y, from_x = (next(source) for _ in range(3))
                out[0, :, at] = plus(kept[0], from_y[...])
                out[1, :, at] = plus(kept[1], from_x[...])

    result = pl.pallas_call(
        body,
        out_shape=out_shape + shapes_of(held, pinned),
        grid_spec=pltpu.PrefetchScalarGridSpec(
            num_scalar_prefetch=1,
            grid=(3,),
            in_specs=in_specs + [ANY] * count,
            out_specs=out_specs + [ANY] * count,
        ),
        input_output_aliases={1 + len(ins) + i: len(out_shape) + i for i in range(count)},
        compiler_params=pltpu.CompilerParams(vmem_limit_bytes=24 * 2**20),
        cost_estimate=SMALL,
    )(order, *ins, *held, *in_hbm(pinned))
    return result[: len(out_shape)], result[len(out_shape) :]


class Gather:
    def __init__(self, shards, order):
        self.shards, self.order = shards, order
        self.plane = lax.axis_size("seq") == 4
        self.gathered = {}
        self.columns, self.near, self.far = {}, {}, {}

    def gather(self, k, axes):
        array = self.shards[k][0]
        if id(array) not in self.gathered:
            self.gathered[id(array)] = lax.all_gather(array, axes, axis=0, tiled=True)
        return self.gathered[id(array)]

    def cut(self, k, value):
        low, high = self.shards[k][1:]
        return value[:, low:high]

    def step(self, *held, take=None, relay=None, begin=None, pinned=()):
        if not self.plane:
            if take is None:
                return (None, *held, *pinned)
            return (self.cut(take, self.gather(take, ("seq", "fsdp"))), *held, *pinned)
        free = [*held] + ([] if relay is None else [*self.near[relay]])
        fixed = [*pinned] + ([] if begin is None else [self.gather(begin, "fsdp")])
        whole = None
        if take is None:
            passed = hold(*free, pinned=fixed)
        else:
            args = (self.columns[take], *self.near[take], *self.far[take])
            whole, *passed = assemble(self.order, *args, free, fixed)
        free, fixed = passed[: len(free)], passed[len(free) :]
        if relay is not None:
            by_x, by_y = self.near[relay] = free[-2:]
            self.far[relay] = flip(by_y[0], "seq", 1), flip(by_x[1], "seq", 2)
        if begin is not None:
            self.gathered[id(self.shards[begin][0])] = fixed[-1]
            column = self.cut(begin, fixed[-1])
            column = column.reshape(2, column.shape[0] // 2, column.shape[1])
            self.columns[begin] = column
            self.near[begin] = flip(column, "seq", 1), flip(column, "seq", 2)
        return (whole, *free[: len(held)], *fixed[: len(pinned)])


class Sums:
    def __init__(self, order):
        self.order = order
        self.plane = lax.axis_size("seq") == 4
        self.terms, self.near, self.far, self.done, self.parts = {}, {}, {}, {}, {}

    def step(self, *held, pinned=(), add=None, pack=None, terms=None, last=(), wait=None, ready=()):
        if not self.plane:
            if pack:
                total = jnp.concatenate(terms, axis=1)
                total = lax.psum_scatter(total, ("seq", "fsdp"), scatter_dimension=0, tiled=True)
                self.parts[pack] = total
            if last:
                self.done[last] = jnp.concatenate([self.parts[name] for name in last], axis=1)
            return (*held, *pinned)
        if pack:
            self.terms[pack] = [v.reshape(8, v.shape[0] // 8, v.shape[1]) for v in terms]
        free = [*held] + ([*self.far[wait][1:]] if wait else [])
        fixed = [*pinned] + [self.done[name] for name in ready]
        outs, passed = sum_step(
            self.order,
            (self.terms.pop(add), *self.near.pop(add)) if add else None,
            add in ("gu0", "gu1"),
            self.terms[pack] if pack else None,
            [self.far.pop(name) for name in last],
            free,
            fixed,
        )
        outs = list(outs)
        free, fixed = passed[: len(free)], passed[len(free) :]
        if wait:
            self.far[wait] = (self.far[wait][0], *free[len(held) :])
        for name, value in zip(ready, fixed[len(pinned) :]):
            self.done[name] = value
        if add:
            to_y, to_x, kept = outs[:3]
            outs = outs[3:]
            self.far[add] = kept, flip(to_y, "seq", 2), flip(to_x, "seq", 1)
        if pack:
            to_x, to_y = outs[:2]
            outs = outs[2:]
            self.near[pack] = flip(to_x, "seq", 1), flip(to_y, "seq", 2)
        if last:
            total = outs[0].reshape(-1, outs[0].shape[2])
            self.done[last] = lax.psum_scatter(total, "fsdp", scatter_dimension=0, tiled=True)
        return (*free[: len(held)], *fixed[: len(pinned)])


def rms(value):
    return lax.rsqrt(jnp.mean(value * value, axis=-1, keepdims=True) + EPSILON)


def split_attention(chunk, qkv_cols):
    gains = chunk[:, qkv_cols : qkv_cols + 2].astype(F32).T
    return chunk[:, :qkv_cols], chunk[:, qkv_cols + GAIN_COLS :], gains[0], gains[1]


def mix(partial, other):
    return partial.astype(F32) + other.astype(F32)


def local(
    inputs,
    cotangent,
    segments,
    w_query,
    w_key,
    w_value,
    w_out,
    w_gate,
    w_up,
    w_down,
    norm_attn,
    norm_mlp,
):
    core = lax.axis_index("section")
    seq_index = lax.axis_index("seq")
    seq_size = lax.axis_size("seq")
    micro, per_dev, rows, width = inputs.shape
    query_width, key_width, ff = w_query.shape[2], w_key.shape[2], w_gate.shape[2]
    parts = micro * per_dev
    chunks = seq_size // parts
    part, chunk = seq_index % parts, seq_index // parts
    tokens = parts * rows
    length = tokens * chunks
    hq, hk = query_width // HEAD // 2, key_width // HEAD // 2
    qkv_cols = (query_width + 2 * key_width) // 2
    core_index = core[None].astype(jnp.int32)
    places = jnp.stack([part, part ^ 1, part ^ 2, part ^ 3]).astype(jnp.int32)
    order = jnp.stack([seq_index, seq_index ^ 1, seq_index ^ 2, seq_index ^ 3]).astype(jnp.int32)

    def chosen(first, second):
        return jnp.where(core == 0, first, second)

    def half(value, index):
        size = value.shape[1] // 2
        return value[:, index * size : (index + 1) * size]

    def shards(halves):
        mine = chosen(halves[0], halves[1])
        theirs = other_core(chosen(halves[1], halves[0]))
        return chosen(mine, theirs), chosen(theirs, mine)

    gains = jnp.pad(jnp.stack([norm_attn[0], norm_mlp[0]], axis=1), ((0, 0), (0, GAIN_COLS - 2)))
    out_t, down_t = w_out[0].T, w_down[0].T

    def attention_pieces(i):
        pieces = [half(w_query[0], i), half(w_key[0], i), half(w_value[0], i), gains]
        return jnp.concatenate(pieces + [half(out_t, i)], axis=1)

    attn_first, attn_second = shards([attention_pieces(0), attention_pieces(1)])
    mlp = (w_gate[0], w_up[0], down_t)
    mlp_first, mlp_second = shards(
        [jnp.concatenate([half(value, i) for value in mlp], axis=1) for i in range(2)]
    )
    attn_first, mlp_first = hold(pinned=(attn_first, mlp_first))
    second = jnp.concatenate([mlp_second, attn_second], axis=1)
    mlp_cols = mlp_second.shape[1]
    chunk_shards = [(attn_first, 0, attn_first.shape[1]), (mlp_first, 0, mlp_cols)]
    chunk_shards += [(second, mlp_cols, second.shape[1]), (second, 0, mlp_cols)]

    piece = rows // 2

    def own_rows(value):
        value = value.reshape(parts, rows, -1)
        return lax.dynamic_slice_in_dim(value, core * piece, piece, 1)

    def sent_rows(own):
        return [flip(pick(own, part ^ step), "seq", step, parts) for step in range(1, parts)]

    def sequence(own, got):
        mine = place(jnp.zeros_like(own), pick(own, part), part)
        for step, value in enumerate(got):
            mine = place(mine, value, part ^ (step + 1))
        other = other_core(mine)
        both = jnp.stack([chosen(mine, other), chosen(other, mine)], axis=1)
        return both.reshape(tokens, both.shape[-1])

    numbers = own_rows(segments).reshape(parts, piece, 1).astype(BF16)
    numbers = jnp.pad(numbers, ((0, 0), (0, 0), (0, 127)))
    own = jnp.concatenate([own_rows(inputs), own_rows(cotangent), numbers], axis=2)
    weights = Gather(chunk_shards, order)
    _, *got = weights.step(*sent_rows(own), begin=0)
    both = sequence(own, got)
    x_first, grad_last = both[:, :width], both[:, width : 2 * width]
    seg_q = both[:, 2 * width].astype(jnp.int32)

    groups = [[i * parts + n for i in range(chunks)] for n in range(parts)]

    def group_gather(value):
        if chunks == 1:
            return value
        return lax.all_gather(value, "seq", axis=0, tiled=True, axis_index_groups=groups)

    def group_scatter(value):
        return lax.psum_scatter(
            value, "seq", scatter_dimension=0, tiled=True, axis_index_groups=groups
        )

    seg_all = group_gather(seg_q)
    pos_q = chunk * tokens + jnp.arange(tokens, dtype=jnp.int32)
    plan = {
        "hq": hq,
        "hk": hk,
        "same": chunks == 1,
        "tables_q": rope_tables(pos_q),
        "tables_k": rope_tables(jnp.arange(length)),
        "seg_q_col": seg_q[:, None],
        "pos_q_col": pos_q[:, None],
        "seg_k_row": seg_all[None, :],
        "seg_q_row": seg_q[None, :],
        "pos_q_row": pos_q[None, :],
        "seg_k_col": seg_all[:, None],
        "gather": group_gather,
        "scatter": group_scatter,
    }

    half_ff = ff // 2
    sums = Sums(order)
    _, x_low, grad_last = weights.step(x_first, grad_last, relay=0)
    attn, x_low = weights.step(x_low, take=0, begin=1)
    kept = []
    for layer in range(2):
        w_qkv, w_out_t, gain_one, gain_two = split_attention(attn, qkv_cols)
        x = x_low.astype(F32)
        scale_one = rms(x)
        normed = (x * scale_one * gain_one).astype(BF16)
        attended = attention_forward(dot(normed, w_qkv), plan)
        transfers = {"relay": 1, "begin": 2} if layer == 0 else {"relay": 3}
        _, out = weights.step(pinned=attended[:1], **transfers)
        attended = (out, *attended[1:])
        own = dot(out, w_out_t, NT).astype(BF16)
        mixed = x + mix(own, other_core(own))
        scale_two = rms(mixed)
        normed_two = (mixed * scale_two * gain_two).astype(BF16)
        transfers = {"take": 1, "relay": 2} if layer == 0 else {"take": 3}
        mlp, normed_two = weights.step(normed_two, **transfers)
        gate, up, hidden, own = mlp_forward(normed_two, mlp)
        if layer == 0:
            next_attn, own = weights.step(own, take=2, begin=3)
        y_low = (mixed + mix(own, other_core(own))).astype(BF16)
        kept.append(
            {
                "w": (attn, mlp),
                "x": x_low,
                "r": scale_one,
                "a": normed,
                "attended": attended,
                "h": mixed.astype(BF16),
                "r2": scale_two,
                "b": normed_two,
                "gate": gate,
                "up": up,
                "hidden": hidden,
            }
        )
        if layer == 0:
            x_low, attn = y_low, next_attn

    grads = [None, None]
    grad_low = grad_last
    for layer in (1, 0):
        keep = kept[layer]
        w_attn, mlp = keep["w"]
        w_qkv, _, gain_one, gain_two = split_attention(w_attn, qkv_cols)
        grad_down = dot(grad_low, keep["hidden"], TN).astype(BF16)
        if layer == 1:
            (grad_low,) = sums.step(grad_low, pack="d1", terms=(grad_down,))
        else:
            (grad_low,) = sums.step(pinned=(grad_low,), add="A1", pack="d0", terms=(grad_down,))
            grads[1] = grad_low
        d_gu, own_two = mlp_backward(grad_low, keep["gate"], keep["up"], mlp)
        if layer == 1:
            own_two, d_gu = sums.step(own_two, pinned=(d_gu,), add="d1")
        else:
            own_two, *y_out.near, d_gu = sums.step(
                own_two, *y_out.near, pinned=(d_gu,), add="d0", wait="A1"
            )
            y_out.onward()
        other = other_core(own_two)
        terms = (dot(keep["b"], d_gu, TN).astype(BF16),)
        if layer == 1:
            (other,) = sums.step(other, pack="gu1", terms=terms, wait="d1")
            y_out = Return(kept[1]["x"], y_low, places, core_index, parts)
        else:
            (other,) = sums.step(other, pack="gu0", terms=terms, last=("A1", "d0"))
        d_mixed, d_out = norm_back(
            own_two,
            other,
            keep["h"],
            keep["r2"],
            gain_two,
            grad_low,
            (w_attn, qkv_cols + GAIN_COLS),
        )
        d_qkv, own_one = attention_backward(keep["attended"], d_out, w_attn, qkv_cols, plan)
        if layer == 1:
            own_one, *y_out.near, d_qkv = sums.step(
                own_one, *y_out.near, pinned=(d_qkv,), add="gu1"
            )
        else:
            own_one, *y_out.far, d_qkv = sums.step(
                own_one, *y_out.far, pinned=(d_qkv,), add="gu0", ready=(("d1", "gu1"),)
            )
        other = other_core(own_one)
        attn_terms = gradient_chunk(
            d_qkv,
            keep["attended"][0],
            (keep["a"], d_mixed, own_one, keep["x"], own_two, keep["h"]),
            (keep["r"], keep["r2"]),
        )
        last = ("d1", "gu1") if layer == 1 else ("gu0",)
        (other,) = sums.step(other, pack="A" + str(layer), terms=(attn_terms,))
        (other,) = sums.step(other, last=last)
        (grad_low,) = norm_back(own_one, other, keep["x"], keep["r"], gain_one, d_mixed)
        grads[layer] = grad_low
    layer_out = y_out.placed()
    *grads, layer_out = sums.step(pinned=(*grads, layer_out), add="A0")
    ready = ("A1", "d0"), ("gu0",)
    grads = sums.step(pinned=grads, last=("A0",), ready=ready)
    x_back = Return(*grads, places, core_index, parts, pinned=True)
    x_back.onward()
    *x_back.far, sums.done[("A0",)] = hold(pinned=(*x_back.far, sums.done[("A0",)]))
    input_grad = x_back.placed()
    layer_out = layer_out.reshape(1, micro, per_dev, rows, width)
    input_grad = input_grad.reshape(1, micro, per_dev, rows, width)

    def owned(first, second):
        keep = chosen(first, second)
        recv = other_core(chosen(second, first))
        return chosen(keep, recv).astype(F32), chosen(recv, keep).astype(F32)

    def joined(halves, start, size):
        at = slice(start, start + size // 2)
        return jnp.concatenate([halves[0][:, at], halves[1][:, at]], axis=1)

    done = sums.done
    cols = attn_terms.shape[1]
    gate, up = (
        owned(done[("gu0",)][:, low : low + half_ff], done[("d1", "gu1")][:, low + half_ff :][:, :half_ff])
        for low in (0, half_ff)
    )
    down = owned(done[("A1", "d0")][:, cols:], done[("d1", "gu1")][:, :half_ff])
    attn = owned(done[("A0",)], done[("A1", "d0")][:, :cols])
    start = query_width // 2
    g_query = joined(attn, 0, query_width)
    g_key = joined(attn, start, key_width)
    g_value = joined(attn, start + key_width // 2, key_width)
    g_out = joined(attn, qkv_cols + GAIN_COLS, query_width).T
    g_gate, g_up, g_down = joined(gate, 0, ff), joined(up, 0, ff), joined(down, 0, ff).T
    gains_owned = (attn[0] + attn[1])[:, qkv_cols : qkv_cols + 2].T
    outs = (g_query, g_key, g_value, g_out, g_gate, g_up, g_down, gains_owned[0], gains_owned[1])
    return (layer_out, input_grad) + tuple(value[None] for value in outs)


def solution(mesh):
    weight_rows = P("section", ("seq", "fsdp"), None)
    weight_cols = P("section", None, ("seq", "fsdp"))
    gain = P("section", ("seq", "fsdp"))
    layer = P("section", None, "fsdp", "seq", None)
    weights = (weight_rows,) * 3 + (weight_cols,) + (weight_rows,) * 2 + (weight_cols,)
    return jax.shard_map(
        local,
        mesh=mesh,
        in_specs=(
            P(None, "fsdp", "seq", None),
            P(None, "fsdp", "seq", None),
            P(None, "fsdp", "seq"),
        )
        + weights
        + (gain, gain),
        out_specs=(layer, layer) + weights + (gain, gain),
        check_vma=False,
    )
```

```python
import functools

import jax
import jax.numpy as jnp
from jax import lax
from jax.experimental import pallas as pl
from jax.experimental.pallas import tpu as pltpu
from jax.sharding import PartitionSpec as P

HEAD = 64
PAIR = 2 * HEAD
EPSILON = 1e-05
ROPE_BASE = 10000.0
NEG = -1e30
GAIN_COLS = 64
LARGE = pl.CostEstimate(flops=1 << 34, bytes_accessed=1024, transcendentals=0)
SMALL = pl.CostEstimate(flops=1024, bytes_accessed=1024, transcendentals=0)
BF16 = jnp.bfloat16
F32 = jnp.float32
NT = (((1,), (1,)), ((), ()))
TN = (((0,), (0,)), ((), ()))
NN = (((1,), (0,)), ((), ()))


def dot(left, right, dims=NN):
    return lax.dot_general(left, right, dims, preferred_element_type=F32)


def swap_halves(value):
    lane = lax.broadcasted_iota(jnp.int32, value.shape, 1)
    ahead = pltpu.roll(value, PAIR - HEAD // 2, 1)
    behind = pltpu.roll(value, HEAD // 2, 1)
    return jnp.where(lane % HEAD < HEAD // 2, ahead, behind)


def rope_tables(positions):
    half = HEAD // 2
    frequency = ROPE_BASE ** (-2.0 * jnp.arange(half, dtype=F32) / HEAD)
    angles = positions.astype(F32)[:, None] * frequency[None, :]
    cosine, sine = jnp.cos(angles), jnp.sin(angles)
    return (
        jnp.concatenate([cosine] * 4, axis=1),
        jnp.concatenate([-sine, sine, -sine, sine], axis=1),
    )


def head_slots(ref, kinds, cos_ref, sin_ref, places, block):
    rows = ref.shape[0]

    def step(i, carry):
        at = pl.ds(pl.multiple_of(i * block, block), block)
        cosine, sine = cos_ref[at, :], sin_ref[at, :]
        for low in range(0, len(kinds), 2):
            pair = range(low, min(low + 2, len(kinds)))
            raw = ref[at, low * HEAD : (pair[-1] + 1) * HEAD].astype(F32)
            if len(pair) == 1:
                raw = jnp.concatenate([raw, raw], axis=1)
            turned = raw
            if any(kinds[slot] != "v" for slot in pair):
                turned = raw * cosine + swap_halves(raw) * sine
            for slot in pair:
                kind = kinds[slot]
                value = raw if kind == "v" else turned
                value = value[:, (slot - low) * HEAD : (slot - low + 1) * HEAD]
                if kind == "q":
                    value = value * 0.125
                dest, index = places[slot]
                dest[index, at, :] = value.astype(BF16)
        return carry

    lax.fori_loop(0, rows // block, step, 0)


def forward_kernel(hq, hk, same, *refs):
    if same:
        q_ref, cosq, sinq, segq, posq, segk, o_ref, qh, kvh, lse_ref, bias, oh, lsec = refs
    else:
        q_ref, kv_ref, cosq, sinq, cosk, sink, segq, posq, segk = refs[:9]
        o_ref, qh, kvh, lse_ref, bias, oh, lsec = refs[9:]
    rows, keys = bias.shape
    block = min(256, rows)
    count = rows // block
    group = hq // hk
    q_kinds, q_places = ["q"] * hq, [(qh, i) for i in range(hq)]
    kv_kinds = ["k"] * hk + ["v"] * hk
    kv_places = [(kvh, i) for i in range(2 * hk)]
    if same:
        head_slots(q_ref, q_kinds + kv_kinds, cosq, sinq, q_places + kv_places, block)
    else:
        head_slots(q_ref, q_kinds, cosq, sinq, q_places, block)
        head_slots(kv_ref, kv_kinds, cosk, sink, kv_places, block)
    for i in range(count):
        at = slice(i * block, (i + 1) * block)
        width = (i + 1) * block if same else keys
        seg_q, pos_q = segq[at, :], posq[at, :]
        seg_k = segk[:, :width]
        pos_k = lax.broadcasted_iota(jnp.int32, (block, width), 1)
        seen = (seg_q == seg_k) & (pos_k <= pos_q) & ((seg_q != 0) | (pos_k == pos_q))
        bias[at, :width] = jnp.where(seen, 0.0, NEG)

    def one_head(h, carry):
        g = lax.div(h, group)
        for i in range(count):
            at = slice(i * block, (i + 1) * block)
            width = (i + 1) * block if same else keys
            scores = dot(qh[h, at, :], kvh[g, :width, :], NT) + bias[at, :width]
            top = jnp.max(scores, axis=1, keepdims=True)
            probs = jnp.exp(scores - top)
            mass = jnp.sum(probs, axis=1, keepdims=True)
            summed = dot(probs.astype(BF16), kvh[hk + g, :width, :])
            oh[h, at, :] = summed / mass
            lane = lax.broadcasted_iota(jnp.int32, (block, 128), 1)
            lsec[at, :] = jnp.where(lane == h, top + jnp.log(mass), lsec[at, :])
        return carry

    lsec[...] = jnp.zeros_like(lsec)
    lax.fori_loop(0, hq, one_head, 0)
    for low in range(0, hq, 2):
        pair = [oh[slot] for slot in range(low, min(low + 2, hq))]
        value = jnp.concatenate(pair, axis=1) if len(pair) == 2 else pair[0]
        o_ref[:, low * HEAD : low * HEAD + value.shape[1]] = value.astype(BF16)
    lse_ref[...] = jnp.transpose(lsec[...])[: lse_ref.shape[0], :]


def unturn(heads, ref, cosine, sine, kinds, block):
    rows = ref.shape[0]

    def step(i, carry):
        at = pl.ds(pl.multiple_of(i * block, block), block)
        cos_part, sin_part = cosine[at, :], sine[at, :]
        for low in range(0, len(kinds), 2):
            pair = range(low, min(low + 2, len(kinds)))
            pieces = [heads[slot][0][heads[slot][1], at, :] for slot in pair]
            raw = jnp.concatenate(pieces if len(pieces) == 2 else pieces * 2, axis=1)
            if kinds[low] != "v":
                turned = raw * cos_part - swap_halves(raw) * sin_part
                if kinds[pair[-1]] == "v":
                    lane = lax.broadcasted_iota(jnp.int32, raw.shape, 1)
                    turned = jnp.where(lane < HEAD, turned, raw)
                raw = turned
            width = len(pieces) * HEAD
            ref[at, low * HEAD : low * HEAD + width] = raw[:, :width].astype(ref.dtype)
        return carry

    lax.fori_loop(0, rows // block, step, 0)


def backward_kernel(hq, hk, same, *refs):
    if same:
        qh, kvh, do_ref, o_ref, lse_ref, cosq, sinq, segq, posq, segk, w_ref = refs[:11]
        dqkv_ref, own_ref, bias, doh, delta, dqs, dks, dvs = refs[11:]
    else:
        qh, kvh, do_ref, o_ref, lse_ref = refs[:5]
        cosq, sinq, cosk, sink, segq, posq, segk = refs[5:12]
        dq_ref, dkv_ref, bias, doh, delta, dqs, dks, dvs = refs[12:]
    keys, rows = bias.shape
    block = min(256, rows)
    count = rows // block
    group = hq // hk
    for i in range(count):
        at = slice(i * block, (i + 1) * block)
        width = (i + 1) * block if same else keys
        seg_q, pos_q = segq[:, at], posq[:, at]
        seg_k = segk[:width, :]
        pos_k = lax.broadcasted_iota(jnp.int32, (width, block), 0)
        seen = (seg_q == seg_k) & (pos_k <= pos_q) & ((seg_q != 0) | (pos_k == pos_q))
        bias[:width, at] = jnp.where(seen, 0.0, NEG)
    for h in range(hq):
        doh[h] = do_ref[:, h * HEAD : (h + 1) * HEAD]
    wide = do_ref.shape[1]
    marks = lax.broadcasted_iota(jnp.int32, (delta.shape[0], wide), 1) // HEAD
    marks = (marks == lax.broadcasted_iota(jnp.int32, marks.shape, 0)).astype(F32)
    products = do_ref[...].astype(F32) * o_ref[...].astype(F32)
    delta[...] = lax.dot_general(
        marks, products, NT, precision=lax.Precision.HIGHEST, preferred_element_type=F32
    )

    def one_group(g, carry):
        dks[g] = jnp.zeros(dks.shape[1:], F32)
        dvs[g] = jnp.zeros(dvs.shape[1:], F32)

        def one_head(j, inner):
            h = g * group + j
            for i in range(count):
                at = slice(i * block, (i + 1) * block)
                width = (i + 1) * block if same else keys
                query, grad = qh[h, at, :], doh[h, at, :]
                key, value = kvh[g, :width, :], kvh[hk + g, :width, :]
                scores = dot(key, query, NT) + bias[:width, at]
                probs = jnp.exp(scores - lse_ref[pl.ds(h, 1), at])
                grad_probs = dot(value, grad, NT)
                grad_scores = (probs * (grad_probs - delta[pl.ds(h, 1), at])).astype(BF16)
                dvs[g, :width, :] += dot(probs.astype(BF16), grad)
                dks[g, :width, :] += dot(grad_scores, query)
                dqs[h, at, :] = dot(grad_scores, key, TN) * 0.125
            return inner

        lax.fori_loop(0, group, one_head, 0)
        return carry

    lax.fori_loop(0, hk, one_group, 0)
    q_heads = [(dqs, i) for i in range(hq)]
    kv_heads = [(dks, i) for i in range(hk)] + [(dvs, i) for i in range(hk)]
    kinds = ["k"] * hk + ["v"] * hk
    if same:
        unturn(q_heads + kv_heads, dqkv_ref, cosq, sinq, ["q"] * hq + kinds, block)

        def project(i, carry):
            at = pl.ds(pl.multiple_of(i * block, block), block)
            weight = w_ref[:, : dqkv_ref.shape[1]]
            own_ref[at, :] = dot(dqkv_ref[at, :], weight, NT).astype(BF16)
            return carry

        lax.fori_loop(0, count, project, 0)
    else:
        unturn(q_heads, dq_ref, cosq, sinq, ["q"] * hq, block)
        unturn(kv_heads, dkv_ref, cosk, sink, kinds, block)


def whole(value):
    zeros = (0,) * len(value.shape)
    return pl.BlockSpec(value.shape, lambda i: zeros, pipeline_mode=pl.Buffered(1))


def in_hbm(arrays):
    return [pltpu.with_memory_space_constraint(value, pltpu.HBM) for value in arrays]


def attention_forward(qkv, plan):
    hq, hk, same = plan["hq"], plan["hk"], plan["same"]
    rows = qkv.shape[0]
    if same:
        keys = rows
        args = [qkv, *plan["tables_q"], plan["seg_q_col"], plan["pos_q_col"], plan["seg_k_row"]]
    else:
        kv_all = plan["gather"](qkv[:, hq * HEAD :])
        keys = kv_all.shape[0]
        args = [qkv[:, : hq * HEAD], kv_all, *plan["tables_q"], *plan["tables_k"]]
        args += [plan["seg_q_col"], plan["pos_q_col"], plan["seg_k_row"]]
    lines = -(-hq // 8) * 8
    out_shape = (
        pltpu.HBM((rows, hq * HEAD), BF16),
        pltpu.HBM((hq, rows, HEAD), BF16),
        pltpu.HBM((2 * hk, keys, HEAD), BF16),
        pltpu.HBM((lines, rows), F32),
    )
    return pl.pallas_call(
        functools.partial(forward_kernel, hq, hk, same),
        out_shape=out_shape,
        grid=(1,),
        in_specs=[whole(value) for value in args],
        out_specs=[whole(value) for value in out_shape],
        scratch_shapes=[
            pltpu.VMEM((rows, keys), F32),
            pltpu.VMEM((hq, rows, HEAD), F32),
            pltpu.VMEM((rows, 128), F32),
        ],
        compiler_params=pltpu.CompilerParams(vmem_limit_bytes=30 * 2**20),
        cost_estimate=SMALL,
    )(*in_hbm(args))


def attention_backward(kept, d_out, w_attn, qkv_cols, plan):
    hq, hk, same = plan["hq"], plan["hk"], plan["same"]
    out, qh, kvh, lse = kept
    rows, keys = out.shape[0], kvh.shape[1]
    args = [qh, kvh, d_out, out, lse, *plan["tables_q"]]
    if not same:
        args += list(plan["tables_k"])
    args += [plan["seg_q_row"], plan["pos_q_row"], plan["seg_k_col"]]
    if same:
        args.append(w_attn)
        out_shape = (
            pltpu.HBM((rows, qkv_cols), BF16),
            jax.ShapeDtypeStruct((rows, w_attn.shape[0]), BF16),
        )
    else:
        out_shape = (
            jax.ShapeDtypeStruct((rows, hq * HEAD), BF16),
            jax.ShapeDtypeStruct((keys, 2 * hk * HEAD), F32),
        )
    result = pl.pallas_call(
        functools.partial(backward_kernel, hq, hk, same),
        out_shape=out_shape,
        grid=(1,),
        in_specs=[whole(value) for value in args],
        out_specs=[whole(value) for value in out_shape],
        scratch_shapes=[
            pltpu.VMEM((keys, rows), F32),
            pltpu.VMEM((hq, rows, HEAD), BF16),
            pltpu.VMEM((lse.shape[0], rows), F32),
            pltpu.VMEM((hq, rows, HEAD), F32),
            pltpu.VMEM((hk, keys, HEAD), F32),
            pltpu.VMEM((hk, keys, HEAD), F32),
        ],
        compiler_params=pltpu.CompilerParams(vmem_limit_bytes=40 * 2**20),
        cost_estimate=SMALL,
    )(*in_hbm(args))
    if same:
        return result
    d_kv = plan["scatter"](result[1]).astype(BF16)
    d_qkv = jnp.concatenate([result[0], d_kv], axis=1)
    return d_qkv, dot(d_qkv, w_attn[:, :qkv_cols], NT).astype(BF16)


def other_core(value):
    return lax.ppermute(value, "section", [(0, 1), (1, 0)])


def place(buffer, block, index):
    return lax.dynamic_update_index_in_dim(buffer, block, index, 0)


def pick(blocks, index):
    return lax.dynamic_index_in_dim(blocks, index, 0, False)


def flip(value, axis, step, group=None):
    size = group or lax.axis_size(axis)
    pairs = [(i, i - i % size + (i % size ^ step)) for i in range(lax.axis_size(axis))]
    return lax.ppermute(value, axis, pairs)


class Return:
    def __init__(self, first, second, places, core, parts, pinned=False):
        self.places, self.core, self.parts = places, core, parts
        self.received = in_hbm if pinned else list
        self.blocks = [v.reshape(2 * parts, -1, v.shape[1]) for v in (first, second)]
        to_x, to_y = self.packed(((1, 0), (3, 0)), ((2, 1), (3, 1)))
        self.near = [flip(to_x, "seq", 1, parts), flip(to_y, "seq", 2, parts)]

    def packed(self, *sends):
        rows, width = self.blocks[0].shape[1:]
        half = rows // 2

        def body(places_ref, core_ref, *refs):
            source, outs = iter(refs[: len(ins)]), refs[len(ins) :]
            for send, out in zip(sends, outs):
                for i, block in enumerate(send):
                    if isinstance(block[0], int):
                        first, second = next(source), next(source)
                        out[i] = jnp.where(core_ref[0] == 0, first[0], second[0])
                    else:
                        out[i] = next(source)[0]

        ins, in_specs = [], []
        for send in sends:
            for place_index, part in send:
                if isinstance(place_index, int):
                    ins += self.received(self.blocks)

                    def index(i, o, c, place_index=place_index, part=part):
                        return (2 * o[place_index] + part, i, 0)

                    in_specs += [pl.BlockSpec((1, half, width), index)] * 2
                else:
                    ins += self.received([place_index])

                    def index(i, o, c, part=part):
                        return (part, i, 0)

                    in_specs.append(pl.BlockSpec((1, half, width), index))
        return pl.pallas_call(
            body,
            out_shape=[jax.ShapeDtypeStruct((len(send), rows, width), BF16) for send in sends],
            grid_spec=pltpu.PrefetchScalarGridSpec(
                num_scalar_prefetch=2,
                grid=(2,),
                in_specs=in_specs,
                out_specs=[
                    pl.BlockSpec((len(send), half, width), lambda i, o, c: (0, i, 0))
                    for send in sends
                ],
            ),
            compiler_params=pltpu.CompilerParams(vmem_limit_bytes=8 * 2**20),
            cost_estimate=SMALL,
        )(self.places, self.core, *ins)

    def onward(self):
        near_x, near_y = self.near
        to_y, to_x = self.packed(((2, 0), (near_x, 1)), ((1, 1), (near_y, 1)))
        self.far = [flip(to_y, "seq", 2, self.parts), flip(to_x, "seq", 1, self.parts)]

    def placed(self):
        near_x, near_y = self.near
        far_y, far_x = self.far
        rows, width = self.blocks[0].shape[1:]
        half, parts = rows // 2, self.parts

        def body(places_ref, core_ref, first_a, second_a, first_b, second_b, nx, ny, fy, fx, out):
            mine = core_ref[0] == 0
            out[2 * places_ref[0]] = jnp.where(mine, first_a[0], second_a[0])
            out[2 * places_ref[0] + 1] = jnp.where(mine, first_b[0], second_b[0])
            out[2 * places_ref[1]] = nx[0]
            out[2 * places_ref[1] + 1] = fx[0]
            out[2 * places_ref[2]] = fy[0]
            out[2 * places_ref[2] + 1] = ny[0]
            out[2 * places_ref[3]] = fy[1]
            out[2 * places_ref[3] + 1] = fx[1]

        def own(part):
            return pl.BlockSpec((1, half, width), lambda i, o, c: (2 * o[0] + part, i, 0))

        def spec(count):
            return pl.BlockSpec((count, half, width), lambda i, o, c: (0, i, 0))

        result = pl.pallas_call(
            body,
            out_shape=jax.ShapeDtypeStruct((2 * parts, rows, width), BF16),
            grid_spec=pltpu.PrefetchScalarGridSpec(
                num_scalar_prefetch=2,
                grid=(2,),
                in_specs=[own(0), own(0), own(1), own(1), spec(1), spec(1), spec(2), spec(2)],
                out_specs=spec(2 * parts),
            ),
            compiler_params=pltpu.CompilerParams(vmem_limit_bytes=12 * 2**20),
            cost_estimate=SMALL,
        )(
            self.places,
            self.core,
            *self.received(self.blocks * 2),
            *self.received((near_x, near_y, far_y, far_x)),
        )
        return result.reshape(parts, 2 * rows, width)


ANY = pl.BlockSpec(memory_space=pl.ANY)
VMEM = pl.BlockSpec(memory_space=pltpu.VMEM)


def shapes_of(arrays, pinned=()):
    kinds = [jax.ShapeDtypeStruct] * len(arrays) + [pltpu.HBM] * len(pinned)
    return [kind(v.shape, v.dtype) for kind, v in zip(kinds, (*arrays, *pinned))]


def hold(*arrays, pinned=()):
    def body(*refs):
        pass

    count = len(arrays) + len(pinned)
    return pl.pallas_call(
        body,
        out_shape=shapes_of(arrays, pinned),
        in_specs=[ANY] * count,
        out_specs=[ANY] * count,
        input_output_aliases={i: i for i in range(count)},
        compiler_params=pltpu.CompilerParams(vmem_limit_bytes=2**20),
        cost_estimate=SMALL,
    )(*arrays, *in_hbm(pinned))


def assemble(order, column, by_x, by_y, far_low, far_high, held, pinned):
    def body(order_ref, col, bx, by, low, high, *refs):
        out = refs[count]
        for i, source in enumerate((col, bx, by)):
            out[pl.ds(2 * order_ref[i], 2)] = source[...]
        out[2 * order_ref[3]] = low[...]
        out[2 * order_ref[3] + 1] = high[...]

    half, cols = column.shape[1:]
    rows = half // 3
    count = len(held) + len(pinned)

    def spec(count):
        return pl.BlockSpec((count, rows, cols), lambda i, o: (0, i, 0))

    single = pl.BlockSpec((rows, cols), lambda i, o: (i, 0))
    result = pl.pallas_call(
        body,
        out_shape=[jax.ShapeDtypeStruct((8, half, cols), column.dtype)]
        + shapes_of(held, pinned),
        grid_spec=pltpu.PrefetchScalarGridSpec(
            num_scalar_prefetch=1,
            grid=(3,),
            in_specs=[spec(2)] * 3 + [single] * 2 + [ANY] * count,
            out_specs=[spec(8)] + [ANY] * count,
        ),
        input_output_aliases={6 + i: 1 + i for i in range(count)},
        compiler_params=pltpu.CompilerParams(vmem_limit_bytes=16 * 2**20),
        cost_estimate=SMALL,
    )(order, column, by_x, by_y, far_low, far_high, *held, *in_hbm(pinned))
    return (result[0].reshape(8 * half, cols), *result[1:])


def gradient_chunk(d_qkv, attended, columns, scales):
    tokens, width = columns[0].shape
    first, last = d_qkv.shape[1], attended.shape[1]
    offset = first + GAIN_COLS
    rows = width // 3

    def body(d_ref, o_ref, a_ref, m_ref, own_a, val_a, own_b, val_b, r_a, r_b, out_ref):
        out_ref[:, :first] = dot(a_ref[...], d_ref[...], TN).astype(BF16)
        lane = lax.broadcasted_iota(jnp.int32, (tokens, GAIN_COLS), 1)
        gains = jnp.zeros((rows, GAIN_COLS), F32)
        for i, (own, val, r) in enumerate(((own_a, val_a, r_a), (own_b, val_b, r_b))):
            product = own[...].astype(F32) * val[...].astype(F32) * r[...]
            unit = jnp.where(lane == i, 1.0, 0.0).astype(BF16)
            gains += dot(product.astype(BF16), unit, TN)
        out_ref[:, first:offset] = gains.astype(BF16)
        out_ref[:, offset:] = dot(m_ref[...], o_ref[...], TN).astype(BF16)

    def part(cols):
        return pl.BlockSpec((tokens, cols), lambda i: (0, 0))

    block = pl.BlockSpec((tokens, rows), lambda i: (0, i))
    return pl.pallas_call(
        body,
        out_shape=pltpu.HBM((width, offset + last), BF16),
        grid=(3,),
        in_specs=[part(first), part(last)] + [block] * 6 + [part(1)] * 2,
        out_specs=pl.BlockSpec((rows, offset + last), lambda i: (i, 0)),
        compiler_params=pltpu.CompilerParams(vmem_limit_bytes=36 * 2**20),
        cost_estimate=LARGE,
    )(*in_hbm((d_qkv, attended, *columns, *scales)))


def norm_back(own, other, value, scale, gain, added, weight=None):
    tokens, width = own.shape
    rows = min(256, tokens)
    low, cols = (weight[1], weight[0].shape[1] - weight[1]) if weight else (0, 0)

    def body(own_ref, other_ref, value_ref, scale_ref, gain_ref, added_ref, *refs):
        grad = (own_ref[...].astype(F32) + other_ref[...].astype(F32)) * gain_ref[...]
        val, r = value_ref[...].astype(F32), scale_ref[...]
        mean = jnp.sum(grad * val, axis=1, keepdims=True) * (1.0 / width)
        result = added_ref[...].astype(F32) + r * grad - val * (r * r * r * mean)
        result = result.astype(BF16)
        refs[-2 if weight else -1][...] = result
        if weight:
            refs[-1][...] = dot(result, refs[0][:, low:]).astype(BF16)

    block = pl.BlockSpec((rows, width), lambda i: (i, 0))
    scales = pl.BlockSpec((rows, 1), lambda i: (i, 0))
    ins = [own, other, value, scale, gain[None, :], added]
    in_specs = [block, block, block, scales, pl.BlockSpec((1, width), lambda i: (0, 0)), block]
    out_shape, out_specs = [pltpu.HBM((tokens, width), BF16)], [block]
    if weight:
        ins.append(weight[0])
        in_specs.append(pl.BlockSpec(weight[0].shape, lambda i: (0, 0)))
        out_shape.append(pltpu.HBM((tokens, cols), BF16))
        out_specs.append(pl.BlockSpec((rows, cols), lambda i: (i, 0)))
    return pl.pallas_call(
        body,
        out_shape=out_shape,
        grid=(tokens // rows,),
        in_specs=in_specs,
        out_specs=out_specs,
        compiler_params=pltpu.CompilerParams(vmem_limit_bytes=24 * 2**20),
        cost_estimate=SMALL,
    )(*in_hbm(ins))


def row_specs(tokens, rows, widths):
    return [pl.BlockSpec((rows, width), lambda i: (i, 0)) for width in widths]


def mlp_forward(normed, weight, hidden_kind):
    tokens, width = normed.shape
    rows, half_ff = min(256, tokens), weight.shape[1] // 3

    def body(b_ref, w_ref, gate_ref, up_ref, hidden_ref, part_ref):
        gate = dot(b_ref[...], w_ref[:, :half_ff])
        up = dot(b_ref[...], w_ref[:, half_ff : 2 * half_ff])
        hidden = (gate * jax.nn.sigmoid(gate) * up).astype(BF16)
        gate_ref[...] = gate.astype(BF16)
        up_ref[...] = up.astype(BF16)
        hidden_ref[...] = hidden
        part_ref[...] = dot(hidden, w_ref[:, 2 * half_ff :], NT).astype(BF16)

    widths = (half_ff, half_ff, half_ff, width)
    return pl.pallas_call(
        body,
        out_shape=[pltpu.HBM((tokens, w), BF16) for w in widths[:2]]
        + [hidden_kind((tokens, half_ff), BF16), jax.ShapeDtypeStruct((tokens, width), BF16)],
        grid=(tokens // rows,),
        in_specs=row_specs(tokens, rows, (width,)) + [VMEM],
        out_specs=row_specs(tokens, rows, widths),
        compiler_params=pltpu.CompilerParams(vmem_limit_bytes=22 * 2**20),
        cost_estimate=SMALL,
    )(normed, weight)


def mlp_backward(grad, gate, up, weight):
    tokens, width = grad.shape
    rows, half_ff = min(256, tokens), weight.shape[1] // 3

    def body(g_ref, gate_ref, up_ref, w_ref, d_gu_ref, part_ref):
        d_hidden = dot(g_ref[...], w_ref[:, 2 * half_ff :])
        z = gate_ref[...].astype(F32)
        sigma = jax.nn.sigmoid(z)
        d_gate = d_hidden * up_ref[...].astype(F32) * sigma * (1.0 + z * (1.0 - sigma))
        d_gate = d_gate.astype(BF16)
        d_up = (d_hidden * z * sigma).astype(BF16)
        d_gu_ref[:, :half_ff] = d_gate
        d_gu_ref[:, half_ff:] = d_up
        part = dot(d_gate, w_ref[:, :half_ff], NT)
        part += dot(d_up, w_ref[:, half_ff : 2 * half_ff], NT)
        part_ref[...] = part.astype(BF16)

    widths = (2 * half_ff, width)
    return pl.pallas_call(
        body,
        out_shape=[
            pltpu.HBM((tokens, widths[0]), BF16),
            jax.ShapeDtypeStruct((tokens, width), BF16),
        ],
        grid=(tokens // rows,),
        in_specs=row_specs(tokens, rows, (width, half_ff, half_ff)) + [VMEM],
        out_specs=row_specs(tokens, rows, widths),
        compiler_params=pltpu.CompilerParams(vmem_limit_bytes=22 * 2**20),
        cost_estimate=SMALL,
    )(*in_hbm((grad, gate, up)), weight)


def sum_step(order, add, add_pinned, pack, last, held, pinned):
    ins, in_specs, out_shape, out_specs = [], [], [], []

    def block(array, which, part, pinned=False):
        rows = array.shape[1] // 3
        (array,) = in_hbm([array]) if pinned else [array]
        spec = pl.BlockSpec((1, rows, array.shape[2]), lambda i, o: (2 * o[which] + part, i, 0))
        ins.append(array)
        in_specs.append(spec)

    def pair(half, cols):
        return pl.BlockSpec((2, half // 3, cols), lambda i, o: (0, i, 0))

    def single(half, cols):
        return pl.BlockSpec((half // 3, cols), lambda i, o: (i, 0))

    def size(terms):
        return terms[0].shape[1], sum(value.shape[2] for value in terms)

    def places(terms):
        low = 0
        for value in terms:
            yield slice(low, low + value.shape[2])
            low += value.shape[2]

    if add is not None:
        terms, got_x, got_y = add
        half, cols = size(terms)
        for value in terms:
            for which, part in ((0, 0), (0, 1), (2, 0), (1, 1)):
                block(value, which, part, add_pinned)
        ins += [got_x, got_y]
        in_specs += [pair(half, cols)] * 2
        out_shape += [jax.ShapeDtypeStruct((half, cols), BF16)] * 2
        out_shape += [jax.ShapeDtypeStruct((2, half, cols), BF16)]
        out_specs += [single(half, cols), single(half, cols), pair(half, cols)]
    if pack is not None:
        half, cols = size(pack)
        for value in pack:
            for which, part in ((1, 0), (3, 0), (2, 1), (3, 1)):
                block(value, which, part)
        out_shape += [jax.ShapeDtypeStruct((2, half, cols), BF16)] * 2
        out_specs += [pair(half, cols)] * 2
    if last:
        for chunk in last:
            half, cols = chunk[1].shape
            ins += list(chunk)
            in_specs += [pair(half, cols), single(half, cols), single(half, cols)]
        half, cols = size([chunk[0] for chunk in last])
        out_shape += [jax.ShapeDtypeStruct((2, half, cols), BF16)]
        out_specs += [pair(half, cols)]

    def plus(left, right):
        return (left.astype(F32) + right.astype(F32)).astype(BF16)

    count = len(held) + len(pinned)

    def body(order_ref, *refs):
        source = iter(refs[: len(ins)])
        target = iter(refs[len(ins) + count :])
        if add is not None:
            blocks = [[next(source) for _ in range(4)] for _ in add[0]]
            gx, gy = next(source), next(source)
            to_y, to_x, kept = (next(target) for _ in range(3))
            for (own_a, own_b, on_a, on_b), at in zip(blocks, places(add[0])):
                to_y[:, at] = plus(on_a[0], gx[1, :, at])
                to_x[:, at] = plus(on_b[0], gy[1, :, at])
                kept[0, :, at] = plus(own_a[0], gx[0, :, at])
                kept[1, :, at] = plus(own_b[0], gy[0, :, at])
        if pack is not None:
            outs = next(target), next(target)
            for at in places(pack):
                for out in outs:
                    for i in range(2):
                        out[i, :, at] = next(source)[0]
        if last:
            out = next(target)
            for at in places([chunk[0] for chunk in last]):
                kept, from_y, from_x = (next(source) for _ in range(3))
                out[0, :, at] = plus(kept[0], from_y[...])
                out[1, :, at] = plus(kept[1], from_x[...])

    result = pl.pallas_call(
        body,
        out_shape=out_shape + shapes_of(held, pinned),
        grid_spec=pltpu.PrefetchScalarGridSpec(
            num_scalar_prefetch=1,
            grid=(3,),
            in_specs=in_specs + [ANY] * count,
            out_specs=out_specs + [ANY] * count,
        ),
        input_output_aliases={1 + len(ins) + i: len(out_shape) + i for i in range(count)},
        compiler_params=pltpu.CompilerParams(vmem_limit_bytes=24 * 2**20),
        cost_estimate=SMALL,
    )(order, *ins, *held, *in_hbm(pinned))
    return result[: len(out_shape)], result[len(out_shape) :]


class Gather:
    def __init__(self, shards, order):
        self.shards, self.order = shards, order
        self.plane = lax.axis_size("seq") == 4
        self.gathered = {}
        self.columns, self.near, self.far = {}, {}, {}

    def gather(self, k, axes):
        array = self.shards[k][0]
        if id(array) not in self.gathered:
            self.gathered[id(array)] = lax.all_gather(array, axes, axis=0, tiled=True)
        return self.gathered[id(array)]

    def cut(self, k, value):
        low, high = self.shards[k][1:]
        return value[:, low:high]

    def step(self, *held, take=None, relay=None, begin=None, pinned=()):
        if not self.plane:
            if take is None:
                return (None, *held, *pinned)
            return (self.cut(take, self.gather(take, ("seq", "fsdp"))), *held, *pinned)
        free = [*held] + ([] if relay is None else [*self.near[relay]])
        fixed = [*pinned] + ([] if begin is None else [self.gather(begin, "fsdp")])
        whole = None
        if take is None:
            passed = hold(*free, pinned=fixed)
        else:
            args = (self.columns[take], *self.near[take], *self.far[take])
            whole, *passed = assemble(self.order, *args, free, fixed)
        free, fixed = passed[: len(free)], passed[len(free) :]
        if relay is not None:
            by_x, by_y = self.near[relay] = free[-2:]
            self.far[relay] = flip(by_y[0], "seq", 1), flip(by_x[1], "seq", 2)
        if begin is not None:
            self.gathered[id(self.shards[begin][0])] = fixed[-1]
            column = self.cut(begin, fixed[-1])
            column = column.reshape(2, column.shape[0] // 2, column.shape[1])
            self.columns[begin] = column
            self.near[begin] = flip(column, "seq", 1), flip(column, "seq", 2)
        return (whole, *free[: len(held)], *fixed[: len(pinned)])


class Sums:
    def __init__(self, order):
        self.order = order
        self.plane = lax.axis_size("seq") == 4
        self.terms, self.near, self.far, self.done, self.parts = {}, {}, {}, {}, {}

    def step(self, *held, pinned=(), add=None, pack=None, terms=None, last=(), wait=None, ready=()):
        if not self.plane:
            if pack:
                total = jnp.concatenate(terms, axis=1)
                total = lax.psum_scatter(total, ("seq", "fsdp"), scatter_dimension=0, tiled=True)
                self.parts[pack] = total
            if last:
                self.done[last] = jnp.concatenate([self.parts[name] for name in last], axis=1)
            return (*held, *pinned)
        if pack:
            self.terms[pack] = [v.reshape(8, v.shape[0] // 8, v.shape[1]) for v in terms]
        free = [*held] + ([*self.far[wait][1:]] if wait else [])
        fixed = [*pinned] + [self.done[name] for name in ready]
        outs, passed = sum_step(
            self.order,
            (self.terms.pop(add), *self.near.pop(add)) if add else None,
            add in ("gu0", "gu1"),
            self.terms[pack] if pack else None,
            [self.far.pop(name) for name in last],
            free,
            fixed,
        )
        outs = list(outs)
        free, fixed = passed[: len(free)], passed[len(free) :]
        if wait:
            self.far[wait] = (self.far[wait][0], *free[len(held) :])
        for name, value in zip(ready, fixed[len(pinned) :]):
            self.done[name] = value
        if add:
            to_y, to_x, kept = outs[:3]
            outs = outs[3:]
            self.far[add] = kept, flip(to_y, "seq", 2), flip(to_x, "seq", 1)
        if pack:
            to_x, to_y = outs[:2]
            outs = outs[2:]
            self.near[pack] = flip(to_x, "seq", 1), flip(to_y, "seq", 2)
        if last:
            total = outs[0].reshape(-1, outs[0].shape[2])
            self.done[last] = lax.psum_scatter(total, "fsdp", scatter_dimension=0, tiled=True)
        return (*free[: len(held)], *fixed[: len(pinned)])


def rms(value):
    return lax.rsqrt(jnp.mean(value * value, axis=-1, keepdims=True) + EPSILON)


def split_attention(chunk, qkv_cols):
    gains = chunk[:, qkv_cols : qkv_cols + 2].astype(F32).T
    return chunk[:, :qkv_cols], chunk[:, qkv_cols + GAIN_COLS :], gains[0], gains[1]


def mix(partial, other):
    return partial.astype(F32) + other.astype(F32)


def local(
    inputs,
    cotangent,
    segments,
    w_query,
    w_key,
    w_value,
    w_out,
    w_gate,
    w_up,
    w_down,
    norm_attn,
    norm_mlp,
):
    core = lax.axis_index("section")
    seq_index = lax.axis_index("seq")
    seq_size = lax.axis_size("seq")
    micro, per_dev, rows, width = inputs.shape
    query_width, key_width, ff = w_query.shape[2], w_key.shape[2], w_gate.shape[2]
    parts = micro * per_dev
    chunks = seq_size // parts
    part, chunk = seq_index % parts, seq_index // parts
    tokens = parts * rows
    length = tokens * chunks
    hq, hk = query_width // HEAD // 2, key_width // HEAD // 2
    qkv_cols = (query_width + 2 * key_width) // 2
    core_index = core[None].astype(jnp.int32)
    places = jnp.stack([part, part ^ 1, part ^ 2, part ^ 3]).astype(jnp.int32)
    order = jnp.stack([seq_index, seq_index ^ 1, seq_index ^ 2, seq_index ^ 3]).astype(jnp.int32)

    def chosen(first, second):
        return jnp.where(core == 0, first, second)

    def half(value, index):
        size = value.shape[1] // 2
        return value[:, index * size : (index + 1) * size]

    def shards(halves):
        mine = chosen(halves[0], halves[1])
        theirs = other_core(chosen(halves[1], halves[0]))
        return chosen(mine, theirs), chosen(theirs, mine)

    gains = jnp.pad(jnp.stack([norm_attn[0], norm_mlp[0]], axis=1), ((0, 0), (0, GAIN_COLS - 2)))
    out_t, down_t = w_out[0].T, w_down[0].T

    def attention_pieces(i):
        pieces = [half(w_query[0], i), half(w_key[0], i), half(w_value[0], i), gains]
        return jnp.concatenate(pieces + [half(out_t, i)], axis=1)

    attn_first, attn_second = shards([attention_pieces(0), attention_pieces(1)])
    mlp = (w_gate[0], w_up[0], down_t)
    mlp_first, mlp_second = shards(
        [jnp.concatenate([half(value, i) for value in mlp], axis=1) for i in range(2)]
    )
    attn_first, mlp_first = hold(pinned=(attn_first, mlp_first))
    second = jnp.concatenate([mlp_second, attn_second], axis=1)
    mlp_cols = mlp_second.shape[1]
    chunk_shards = [(attn_first, 0, attn_first.shape[1]), (mlp_first, 0, mlp_cols)]
    chunk_shards += [(second, mlp_cols, second.shape[1]), (second, 0, mlp_cols)]

    piece = rows // 2

    def own_rows(value):
        value = value.reshape(parts, rows, -1)
        return lax.dynamic_slice_in_dim(value, core * piece, piece, 1)

    def sent_rows(own):
        return [flip(pick(own, part ^ step), "seq", step, parts) for step in range(1, parts)]

    def sequence(own, got):
        mine = place(jnp.zeros_like(own), pick(own, part), part)
        for step, value in enumerate(got):
            mine = place(mine, value, part ^ (step + 1))
        other = other_core(mine)
        both = jnp.stack([chosen(mine, other), chosen(other, mine)], axis=1)
        return both.reshape(tokens, both.shape[-1])

    numbers = own_rows(segments).reshape(parts, piece, 1).astype(BF16)
    numbers = jnp.pad(numbers, ((0, 0), (0, 0), (0, 127)))
    own = jnp.concatenate([own_rows(inputs), own_rows(cotangent), numbers], axis=2)
    weights = Gather(chunk_shards, order)
    _, *got = weights.step(*sent_rows(own), begin=0)
    both = sequence(own, got)
    x_first, grad_last = both[:, :width], both[:, width : 2 * width]
    seg_q = both[:, 2 * width].astype(jnp.int32)

    groups = [[i * parts + n for i in range(chunks)] for n in range(parts)]

    def group_gather(value):
        if chunks == 1:
            return value
        return lax.all_gather(value, "seq", axis=0, tiled=True, axis_index_groups=groups)

    def group_scatter(value):
        return lax.psum_scatter(
            value, "seq", scatter_dimension=0, tiled=True, axis_index_groups=groups
        )

    seg_all = group_gather(seg_q)
    pos_q = chunk * tokens + jnp.arange(tokens, dtype=jnp.int32)
    plan = {
        "hq": hq,
        "hk": hk,
        "same": chunks == 1,
        "tables_q": rope_tables(pos_q),
        "tables_k": rope_tables(jnp.arange(length)),
        "seg_q_col": seg_q[:, None],
        "pos_q_col": pos_q[:, None],
        "seg_k_row": seg_all[None, :],
        "seg_q_row": seg_q[None, :],
        "pos_q_row": pos_q[None, :],
        "seg_k_col": seg_all[:, None],
        "gather": group_gather,
        "scatter": group_scatter,
    }

    half_ff = ff // 2
    sums = Sums(order)
    _, x_low, grad_last = weights.step(x_first, grad_last, relay=0)
    attn, x_low = weights.step(x_low, take=0, begin=1)
    kept = []
    for layer in range(2):
        w_qkv, w_out_t, gain_one, gain_two = split_attention(attn, qkv_cols)
        x = x_low.astype(F32)
        scale_one = rms(x)
        normed = (x * scale_one * gain_one).astype(BF16)
        attended = attention_forward(dot(normed, w_qkv), plan)
        transfers = {"relay": 1, "begin": 2} if layer == 0 else {"relay": 3}
        _, out = weights.step(pinned=attended[:1], **transfers)
        attended = (out, *attended[1:])
        own = dot(out, w_out_t, NT).astype(BF16)
        mixed = x + mix(own, other_core(own))
        scale_two = rms(mixed)
        normed_two = (mixed * scale_two * gain_two).astype(BF16)
        transfers = {"take": 1, "relay": 2} if layer == 0 else {"take": 3}
        mlp, normed_two = weights.step(normed_two, **transfers)
        gate, up, hidden, own = mlp_forward(
            normed_two, mlp, pltpu.HBM if layer == 0 else jax.ShapeDtypeStruct
        )
        if layer == 0:
            next_attn, own = weights.step(own, take=2, begin=3)
        y_low = (mixed + mix(own, other_core(own))).astype(BF16)
        kept.append(
            {
                "w": (attn, mlp),
                "x": x_low,
                "r": scale_one,
                "a": normed,
                "attended": attended,
                "h": mixed.astype(BF16),
                "r2": scale_two,
                "b": normed_two,
                "gate": gate,
                "up": up,
                "hidden": hidden,
            }
        )
        if layer == 0:
            x_low, attn = y_low, next_attn

    grads = [None, None]
    grad_low = grad_last
    for layer in (1, 0):
        keep = kept[layer]
        w_attn, mlp = keep["w"]
        w_qkv, _, gain_one, gain_two = split_attention(w_attn, qkv_cols)
        grad_down = dot(grad_low, keep["hidden"], TN).astype(BF16)
        if layer == 1:
            (grad_low,) = sums.step(grad_low, pack="d1", terms=(grad_down,))
        else:
            (grad_low,) = sums.step(pinned=(grad_low,), add="A1", pack="d0", terms=(grad_down,))
            grads[1] = grad_low
        d_gu, own_two = mlp_backward(grad_low, keep["gate"], keep["up"], mlp)
        if layer == 1:
            own_two, d_gu = sums.step(own_two, pinned=(d_gu,), add="d1")
        else:
            own_two, *y_out.near, d_gu = sums.step(
                own_two, *y_out.near, pinned=(d_gu,), add="d0", wait="A1"
            )
            y_out.onward()
        other = other_core(own_two)
        terms = (dot(keep["b"], d_gu, TN).astype(BF16),)
        if layer == 1:
            (other,) = sums.step(other, pack="gu1", terms=terms, wait="d1")
            y_out = Return(kept[1]["x"], y_low, places, core_index, parts)
        else:
            (other,) = sums.step(other, pack="gu0", terms=terms, last=("A1", "d0"))
        d_mixed, d_out = norm_back(
            own_two,
            other,
            keep["h"],
            keep["r2"],
            gain_two,
            grad_low,
            (w_attn, qkv_cols + GAIN_COLS),
        )
        d_qkv, own_one = attention_backward(keep["attended"], d_out, w_attn, qkv_cols, plan)
        if layer == 1:
            own_one, *y_out.near, d_qkv = sums.step(
                own_one, *y_out.near, pinned=(d_qkv,), add="gu1"
            )
        else:
            own_one, *y_out.far, d_qkv = sums.step(
                own_one, *y_out.far, pinned=(d_qkv,), add="gu0", ready=(("d1", "gu1"),)
            )
        other = other_core(own_one)
        attn_terms = gradient_chunk(
            d_qkv,
            keep["attended"][0],
            (keep["a"], d_mixed, own_one, keep["x"], own_two, keep["h"]),
            (keep["r"], keep["r2"]),
        )
        last = ("d1", "gu1") if layer == 1 else ("gu0",)
        (other,) = sums.step(other, pack="A" + str(layer), terms=(attn_terms,))
        (other,) = sums.step(other, last=last)
        (grad_low,) = norm_back(own_one, other, keep["x"], keep["r"], gain_one, d_mixed)
        grads[layer] = grad_low
    layer_out = y_out.placed()
    *grads, layer_out = sums.step(pinned=(*grads, layer_out), add="A0")
    ready = ("A1", "d0"), ("gu0",)
    grads = sums.step(pinned=grads, last=("A0",), ready=ready)
    x_back = Return(*grads, places, core_index, parts, pinned=True)
    x_back.onward()
    *x_back.far, sums.done[("A0",)] = hold(pinned=(*x_back.far, sums.done[("A0",)]))
    input_grad = x_back.placed()
    layer_out = layer_out.reshape(1, micro, per_dev, rows, width)
    input_grad = input_grad.reshape(1, micro, per_dev, rows, width)

    def owned(first, second):
        keep = chosen(first, second)
        recv = other_core(chosen(second, first))
        return chosen(keep, recv).astype(F32), chosen(recv, keep).astype(F32)

    def joined(halves, start, size):
        at = slice(start, start + size // 2)
        return jnp.concatenate([halves[0][:, at], halves[1][:, at]], axis=1)

    done = sums.done
    cols = attn_terms.shape[1]
    gate, up = (
        owned(done[("gu0",)][:, low : low + half_ff], done[("d1", "gu1")][:, low + half_ff :][:, :half_ff])
        for low in (0, half_ff)
    )
    down = owned(done[("A1", "d0")][:, cols:], done[("d1", "gu1")][:, :half_ff])
    attn = owned(done[("A0",)], done[("A1", "d0")][:, :cols])
    start = query_width // 2
    g_query = joined(attn, 0, query_width)
    g_key = joined(attn, start, key_width)
    g_value = joined(attn, start + key_width // 2, key_width)
    g_out = joined(attn, qkv_cols + GAIN_COLS, query_width).T
    g_gate, g_up, g_down = joined(gate, 0, ff), joined(up, 0, ff), joined(down, 0, ff).T
    gains_owned = (attn[0] + attn[1])[:, qkv_cols : qkv_cols + 2].T
    outs = (g_query, g_key, g_value, g_out, g_gate, g_up, g_down, gains_owned[0], gains_owned[1])
    return (layer_out, input_grad) + tuple(value[None] for value in outs)


def solution(mesh):
    weight_rows = P("section", ("seq", "fsdp"), None)
    weight_cols = P("section", None, ("seq", "fsdp"))
    gain = P("section", ("seq", "fsdp"))
    layer = P("section", None, "fsdp", "seq", None)
    weights = (weight_rows,) * 3 + (weight_cols,) + (weight_rows,) * 2 + (weight_cols,)
    return jax.shard_map(
        local,
        mesh=mesh,
        in_specs=(
            P(None, "fsdp", "seq", None),
            P(None, "fsdp", "seq", None),
            P(None, "fsdp", "seq"),
        )
        + weights
        + (gain, gain),
        out_specs=(layer, layer) + weights + (gain, gain),
        check_vma=False,
    )
```
